32 devices in a mesh: section: 8 (over z, core), tensor: 4 (over y, x).
Axes of the slice: x: 2, y: 2, z: 4, core: 2. Of those that a mesh axis runs over, the one named last changes fastest.
Arguments:
- activations: bfloat16 [8, 512, 4096], P('section', None, 'tensor'), may hold values from -48 to 48
- gain: bfloat16 [8, 4096], P('section', 'tensor'), may hold values from 0.5 to 1.5
- w_query: bfloat16 [8, 4096, 4096], P('section', None, 'tensor'), may hold values from -0.0625 to 0.0625
- w_kv: bfloat16 [8, 1024, 4096], P('section', 'tensor'), may hold values from -1.8782524 to 1.8782524
- segments: int32 [8, 512], replicated, may hold values from 0 to 31, never falling along the last dimension, each value on 1 to 128 neighbouring positions
- pool: bfloat16 [16, 128, 4096], P('section', None, 'tensor'), may hold values from -48 to 48
- row_ids: int32 [32], replicated, may hold values from 0 to 15, as said below
- row_lengths: int32 [32], replicated, may hold values from 1 to 128, 512 in all
Outputs:
- after_first: bfloat16 [8, 512, 4096], P('section', None, 'tensor')
- after_second: bfloat16 [8, 512, 4096], P('section', None, 'tensor')
The draws below stay inside these ranges and needn't reach their ends.
Inputs may be any that keep to these rules, and one draw needn't show every extreme that they name: `row_ids`: every block of 2 consecutive ids, the rows of one buffer host, is named at least once; ids may repeat.
All inputs are finite; a program needn't handle non-finite values.
Results may differ from the reference program's by a relative error of at most 0.01.
Values may be sent and summed in bfloat16 or wider, within the bound.
A program may use at most 64 MiB of HBM per device.

```python
import math
import jax
import jax.numpy as jnp
import numpy as np
from jax import lax

D = 4096
HEADS = 32
KV_HEADS = 4
HEAD_DIM = 128
TOKENS_MB = 512
ROWS_MB = 32
ROW_MAX = 128
HOST_ROWS = 2
LAYERS = 8
POOL_ROWS = 16


def rough_field(key, lead_dim, row_count, col_count):
    sub_keys = jax.random.split(key, 4)
    col_place = jnp.arange(col_count, dtype=jnp.float32) / col_count
    base_vals = jnp.clip(jax.random.normal(sub_keys[0], (lead_dim, row_count, col_count), jnp.float32), -4.0, 4.0)
    col_trend = jnp.exp(math.log(3.0) * (col_place - 0.5))
    row_scale = jnp.exp(jax.random.uniform(sub_keys[2], (lead_dim, row_count, 1), jnp.float32, math.log(0.3), math.log(3.0)))
    col_scale = jnp.exp(jax.random.uniform(sub_keys[3], (lead_dim, 1, col_count), jnp.float32, -0.5 * math.log(10.0), 0.5 * math.log(10.0)))
    values_out = base_vals * row_scale * col_scale * col_trend[None, None, :]
    return jnp.clip(values_out, -48.0, 48.0)


def query_head(key, head_number):
    raw_vals = jax.random.normal(jax.random.fold_in(key, 100 + head_number), (LAYERS, D, HEAD_DIM), jnp.float32)
    return jnp.clip(raw_vals, -4.0, 4.0) * D ** (-0.5)


def draw_activations(key, part):
    return rough_field(jax.random.fold_in(key, 1), LAYERS, TOKENS_MB, D).astype(jnp.bfloat16)


def draw_pool(key, part):
    return rough_field(jax.random.fold_in(key, 2), POOL_ROWS, ROW_MAX, D).astype(jnp.bfloat16)


def draw_w_query(key, part):
    blocks = [query_head(key, head_number) for head_number in range(HEADS)]
    return jnp.concatenate(blocks, axis=2).astype(jnp.bfloat16)


def draw_w_kv(key, part):
    raw_vals = jax.random.normal(jax.random.fold_in(key, 5), (LAYERS, 2 * KV_HEADS * HEAD_DIM, D), jnp.float32)
    weights_out = jnp.clip(raw_vals, -4.0, 4.0) * D ** (-0.5)
    return weights_out.astype(jnp.bfloat16)


def draw_row_ids(key, part):
    sub_keys = jax.random.split(jax.random.fold_in(key, 9), 4)
    host_count = POOL_ROWS // HOST_ROWS
    extra_count = ROWS_MB - host_count
    hosts_first = jax.random.permutation(sub_keys[0], host_count).astype(jnp.int32)
    hosts_extra = jax.random.randint(sub_keys[1], (extra_count,), 0, host_count).astype(jnp.int32)
    local_first = jnp.where(hosts_first == 0, 0, HOST_ROWS - 1).astype(jnp.int32)
    local_extra = jax.random.randint(sub_keys[2], (extra_count,), 0, HOST_ROWS).astype(jnp.int32)
    shuffle_order = jax.random.permutation(sub_keys[3], ROWS_MB)
    host_all = jnp.concatenate([hosts_first, hosts_extra])[shuffle_order]
    local_all = jnp.concatenate([local_first, local_extra])[shuffle_order]
    return (host_all * HOST_ROWS + local_all).astype(jnp.int32)


def split_up(amount, total, most, lean):
    loads = [(1 << 20) // math.isqrt(rank ** lean) + 1 for rank in range(2, amount + 1)]
    rest, holding = total - most - (amount - 1), [1] * (amount - 1)
    while rest > 0:
        candidates = [i for i in range(amount - 1) if holding[i] < most]
        whole, budget = sum([loads[i] for i in candidates]), rest
        for i in candidates:
            addition = min(most - holding[i], max(1, budget * loads[i] // whole), rest)
            holding[i] = holding[i] + addition
            rest = rest - addition
    return np.array([most] + holding)


def ragged_sizes(key, number_of, total, limit, lean):
    if number_of == 2:
        one = jax.random.randint(key, (), max(1, total - limit), min(limit, total - 1) + 1)
        return jnp.stack([one, total - one])
    tallies = jnp.asarray(split_up(number_of, total, limit, lean), jnp.int32)
    couples = (number_of - 1) // 2
    source_of, receiver = tallies[1:1 + 2 * couples:2], tallies[2:2 + 2 * couples:2]
    slack = jnp.minimum(source_of - 1, limit - receiver)
    moved = jax.random.randint(jax.random.fold_in(key, 1), (couples,), 0, 1 << 20) % (slack + 1)
    tallies = tallies.at[1:1 + 2 * couples:2].set(source_of - moved).at[2:2 + 2 * couples:2].set(receiver + moved)
    return tallies[jax.random.permutation(jax.random.fold_in(key, 2), number_of)]


def setup_inputs(seed: int = 0) -> dict:
    arg_keys = jax.random.split(jax.random.key(seed), 9)
    activations = draw_activations(jax.random.fold_in(arg_keys[8], 71), 0)
    gain = jnp.clip(1.0 + 0.1 * jax.random.normal(arg_keys[1], (LAYERS, D), jnp.float32), 0.5, 1.5).astype(jnp.bfloat16)
    w_query = draw_w_query(jax.random.fold_in(arg_keys[8], 71), 0)
    w_kv = draw_w_kv(jax.random.fold_in(arg_keys[8], 71), 0)
    segments = jax.vmap(lambda own: jnp.searchsorted(jnp.cumsum(ragged_sizes(own, ROWS_MB, TOKENS_MB, ROW_MAX, 2)), jnp.arange(TOKENS_MB), side="right"))(jax.random.split(arg_keys[4], LAYERS)).reshape((LAYERS, TOKENS_MB)).astype(jnp.int32)
    pool = draw_pool(jax.random.fold_in(arg_keys[8], 71), 0)
    row_ids = draw_row_ids(jax.random.fold_in(arg_keys[8], 71), 0)
    row_lengths = ragged_sizes(arg_keys[7], ROWS_MB, TOKENS_MB, ROW_MAX, 2).astype(jnp.int32)
    return dict(activations=activations, gain=gain, w_query=w_query, w_kv=w_kv, segments=segments, pool=pool, row_ids=row_ids, row_lengths=row_lengths)


norm_eps = 1e-05
masked_score = -1e+30

def attend_layer(inputs, gain_row, query_weight, keyval_weight, seg_ids):
    row_count = inputs.shape[0]
    wide_inputs = inputs.astype(jnp.float32)
    mean_square = lax.optimization_barrier(jnp.mean(wide_inputs * wide_inputs, axis=1, keepdims=True))
    normed = (wide_inputs * lax.rsqrt(mean_square + norm_eps) * gain_row.astype(jnp.float32)[None, :]).astype(jnp.bfloat16)
    query = jnp.dot(normed, query_weight, preferred_element_type=jnp.float32).astype(jnp.bfloat16)
    keyval = jnp.dot(normed, keyval_weight.T, preferred_element_type=jnp.float32).astype(jnp.bfloat16)
    query = query.reshape(row_count, HEADS, HEAD_DIM).astype(jnp.float32)
    keyval = keyval.reshape(row_count, KV_HEADS, 2, HEAD_DIM).astype(jnp.float32)
    group_size = HEADS // KV_HEADS
    key_heads = jnp.repeat(keyval[:, :, 0], group_size, axis=1)
    value_heads = jnp.repeat(keyval[:, :, 1], group_size, axis=1)
    positions = jnp.arange(row_count, dtype=jnp.int32)
    allowed = (seg_ids[:, None] == seg_ids[None, :]) & (positions[None, :] <= positions[:, None])
    scores = jnp.einsum('rhd,shd->hrs', query, key_heads, precision=lax.Precision.HIGHEST) * HEAD_DIM ** (-0.5)
    scores = jnp.where(allowed[None, :, :], scores, masked_score)
    weights = jax.nn.softmax(scores, axis=-1).astype(jnp.bfloat16)
    context = jnp.einsum('hrs,shd->rhd', weights.astype(jnp.float32), value_heads, precision=lax.Precision.HIGHEST)
    context = context.astype(jnp.bfloat16).reshape(row_count, HEADS * HEAD_DIM)
    return (wide_inputs + context.astype(jnp.float32)).astype(jnp.bfloat16)

def run_sections(packed):
    return attend_layer(packed[0], packed[1], packed[2], packed[3], packed[4])

def reference(activations, gain, w_query, w_kv, segments, pool, row_ids, row_lengths):
    after_first = lax.map(run_sections, (activations, gain, w_query, w_kv, segments))
    token_count = activations.shape[1]
    ends = jnp.cumsum(row_lengths).astype(jnp.int32)
    positions = jnp.arange(token_count, dtype=jnp.int32)
    slot = lax.optimization_barrier(jnp.sum((positions[:, None] >= ends[None, :]).astype(jnp.int32), axis=1)).astype(jnp.int32)
    offset = (positions - ends[slot] + row_lengths[slot]).astype(jnp.int32)
    source = (row_ids[slot] * pool.shape[1] + offset).astype(jnp.int32)
    fresh = pool.reshape(-1, pool.shape[2])[source]
    second_inputs = jnp.concatenate([fresh[None], after_first[:-1]], axis=0)
    second_segments = jnp.concatenate([slot[None], segments[:-1]], axis=0).astype(jnp.int32)
    after_second = lax.map(run_sections, (second_inputs, gain, w_query, w_kv, second_segments))
    return (after_first, after_second)
```

```python
import functools

import jax
import jax.numpy as jnp
from jax import lax
from jax.experimental import pallas as pl
from jax.experimental.pallas import tpu as pltpu
from jax.sharding import PartitionSpec as P

D = 4096
HEADS = 32
KV_HEADS = 4
HEAD_DIM = 128


norm_eps = 1e-05
masked_score = -1e30


def partner_2(block, axis, distance):
    count = lax.axis_size(axis)
    route = []
    for low in range(count):
        high = low | 1 << distance
        if high != low and high < count:
            route += [(low, high), (high, low)]
    return lax.ppermute(block, axis, route)


def from_behind(block, axis, distance):
    devices = range(lax.axis_size(axis))
    route = [(i - distance, i) for i in devices if i - distance in devices]
    return lax.ppermute(block, axis, route)


def attend(inputs, gain_cols, query_weight, keyval_weight, seg_ids, tensor_index):
    row_count, col_count = inputs.shape
    wide_inputs = inputs.astype(jnp.float32)
    square_total = lax.psum(jnp.sum(wide_inputs * wide_inputs, axis=1), "tensor")
    row_scale = lax.rsqrt(square_total / D + norm_eps)
    normed = (wide_inputs * row_scale[:, None] * gain_cols.astype(jnp.float32)[None, :]).astype(
        jnp.bfloat16
    )
    part_cols = lax.all_gather(normed, "tensor", axis=1, tiled=True)
    query_part = jnp.dot(part_cols, query_weight, preferred_element_type=jnp.float32)
    keyval_part = lax.dot_general(
        keyval_weight, part_cols, (((1,), (1,)), ((), ())), preferred_element_type=jnp.float32
    )
    query = query_part.astype(jnp.bfloat16)
    keyval = keyval_part.astype(jnp.bfloat16)
    heads_here = query_weight.shape[1] // HEAD_DIM
    group_size = HEADS // KV_HEADS
    group_devices = group_size // heads_here
    head_block = keyval
    for bit_number in range(group_devices.bit_length() - 1):
        partner = partner_2(head_block, "tensor", bit_number)
        is_lower = tensor_index // (1 << bit_number) % 2 == 0
        head_block = jnp.where(
            is_lower,
            jnp.concatenate([head_block, partner], axis=0),
            jnp.concatenate([partner, head_block], axis=0),
        )
    keys_cols = head_block[:HEAD_DIM]
    values_cols = head_block[HEAD_DIM:]
    query_heads = query.reshape(row_count, heads_here, HEAD_DIM)
    scores = jnp.einsum(
        "rhd,ds->hrs", query_heads, keys_cols, preferred_element_type=jnp.float32
    ) * HEAD_DIM ** (-0.5)
    positions = jnp.arange(row_count, dtype=jnp.int32)
    allowed = (seg_ids[:, None] == seg_ids[None, :]) & (positions[None, :] <= positions[:, None])
    scores = jnp.where(allowed[None, :, :], scores, masked_score)
    weights = jax.nn.softmax(scores, axis=-1).astype(jnp.bfloat16)
    context = jnp.einsum("hrs,ds->rhd", weights, values_cols, preferred_element_type=jnp.float32)
    context = context.astype(jnp.bfloat16).reshape(row_count, col_count)
    return (wide_inputs + context.astype(jnp.float32)).astype(jnp.bfloat16)


def pick_rows(running, host_rows, source):
    flat_rows = host_rows.reshape(-1, host_rows.shape[2])
    inside = (source >= 0) & (source < flat_rows.shape[0])
    taken = jnp.take(flat_rows, jnp.clip(source, 0, flat_rows.shape[0] - 1), axis=0)
    return jnp.where(inside[:, None], taken, running)


def per_device(activations, gain, w_query, w_kv, segments, pool, row_ids, row_lengths):
    section_index = lax.axis_index("section")
    tensor_index = lax.axis_index("tensor")
    token_count = activations.shape[1]
    col_count = activations.shape[2]
    own_segments = lax.dynamic_index_in_dim(segments, section_index, 0, keepdims=False)
    after_first = attend(activations[0], gain[0], w_query[0], w_kv[0], own_segments, tensor_index)[
        None
    ]
    ends = jnp.cumsum(row_lengths)
    positions = jnp.arange(token_count, dtype=jnp.int32)
    slot = jnp.sum((positions[:, None] >= ends[None, :]).astype(jnp.int32), axis=1)
    slot_match = slot[:, None] == jnp.arange(row_ids.shape[0], dtype=jnp.int32)[None, :]
    slot_start = jnp.sum(jnp.where(slot_match, (ends - row_lengths)[None, :], 0), axis=1)
    slot_row = jnp.sum(jnp.where(slot_match, row_ids[None, :], 0), axis=1)
    source = slot_row * pool.shape[1] + positions - slot_start
    empty_rows = jnp.zeros((token_count, col_count), jnp.bfloat16)
    fresh = pick_rows(empty_rows, lax.all_gather(pool, "section", axis=0, tiled=True), source)
    handed = from_behind(after_first, "section", 1)
    second_inputs = jnp.where(section_index == 0, fresh[None], handed)
    prior_segments = lax.dynamic_index_in_dim(
        segments, jnp.maximum(section_index - 1, 0), 0, keepdims=False
    )
    second_segments = jnp.where(section_index == 0, slot, prior_segments)
    after_second = attend(
        second_inputs[0], gain[0], w_query[0], w_kv[0], second_segments, tensor_index
    )[None]
    return (after_first, after_second)


BLOCK = 128
MESH = pl.DeviceIdType.MESH


def relay_kernel(
    sections, hosts_rows, slots,
    a_ref, gain_ref, wq_ref, wkv_ref, seg_ref, pool_ref, ids_ref, len_ref,
    out1_ref, out2_ref,
    got, weight, kv_raw, gains, normed, query, keys, values, seg_rows, src_rows,
    pool_rows, above, below, result,
    own_send, own_recv, fwd_send, fwd_recv, gain_send, gain_recv, hand_send, hand_recv,
    x_sem, wq_sem, wkv_sem, pool_sem, mate_send, mate_recv, sum_send, sum_recv, out_sem,
):
    sec = lax.axis_index("section")
    ten = lax.axis_index("tensor")
    blocks = a_ref.shape[1] // BLOCK
    steps = 2 * blocks
    cols = a_ref.shape[2]
    over_x = ten + 1 - 2 * (ten % 2)
    over_y = ten + 2 - 4 * (ten // 2)
    peers = (ten, over_x, over_y, 3 - ten)
    even = sec % 2 == 0
    top = sections - 2

    x_copies = [
        pltpu.make_async_copy(
            a_ref.at[0, pl.ds(k * BLOCK, BLOCK)], got.at[k, 0], x_sem.at[k]
        )
        for k in range(blocks)
    ]
    wq_copies, wkv_copies = [], []
    for r in range(4):
        part = pl.ds(pl.multiple_of(peers[r] * cols, cols), cols)
        wq_copies.append(
            pltpu.make_async_copy(
                wq_ref.at[0, part], weight.at[pl.ds(r * cols, cols), pl.ds(0, cols)], wq_sem.at[r]
            )
        )
        wkv_copies.append(
            pltpu.make_async_copy(wkv_ref.at[0, :, part], kv_raw.at[r], wkv_sem.at[r])
        )
    pool_copy = pltpu.make_async_copy(pool_ref, pool_rows.at[0], pool_sem)
    x_copies[0].start()
    for copy in wkv_copies + wq_copies + x_copies[1:]:
        copy.start()

    @pl.when(even)
    def _():
        pool_copy.start()

    barrier = pltpu.get_barrier_semaphore()
    for r in (1, 2, 3):
        pl.semaphore_signal(barrier, inc=1, device_id=(sec, peers[r]), device_id_type=MESH)

    def greet(condition, other):
        @pl.when(condition)
        def _():
            pl.semaphore_signal(barrier, inc=1, device_id=(other, ten), device_id_type=MESH)

    greet(sec > 0, sec - 1)
    greet(sec < sections - 1, sec + 1)
    greet(even & (sec > 1), sec - 2)
    greet(even & (sec < top), sec + 2)
    others = 3
    for condition in (sec > 0, sec < sections - 1, even & (sec > 1), even & (sec < top)):
        others = others + jnp.where(condition, 1, 0)
    pl.semaphore_wait(barrier, others)

    def remote(src, dst, send_sem, recv_sem, device):
        return pltpu.make_async_remote_copy(
            src_ref=src, dst_ref=dst, send_sem=send_sem, recv_sem=recv_sem,
            device_id=device, device_id_type=MESH,
        )

    def own_copy(src, b, way):
        return remote(
            src, got.at[b, 1 + way], own_send.at[b, way], own_recv.at[b, way],
            (sec, peers[1 + way]),
        )

    half = BLOCK // 2

    def forward_copy(b, way):
        rows = pl.ds(way * half, half)
        return remote(
            got.at[b, 1 + way, rows], got.at[b, 3, rows], fwd_send.at[b, way],
            fwd_recv.at[b, way], (sec, peers[2 - way]),
        )

    def hand_copy(k):
        return remote(
            result.at[k], got.at[blocks + k, 0], hand_send.at[k], hand_recv.at[k], (sec + 1, ten)
        )

    def sum_copy(k):
        return remote(below.at[k], above.at[k], sum_send.at[k], sum_recv.at[k], (sec - 2, ten))

    def gain_copy(r):
        return remote(
            gains.at[0], gains.at[r], gain_send.at[r - 1], gain_recv.at[r - 1], (sec, peers[r])
        )

    mate_copy = remote(pool_ref, pool_rows.at[1], mate_send, mate_recv, (sec - 1, ten))

    for k in range(2):
        for way in range(2):
            own_copy(a_ref.at[0, pl.ds(k * BLOCK, BLOCK)], k, way).start()
    gains[0] = jnp.broadcast_to(gain_ref[...], gains.shape[1:])
    for r in (1, 2, 3):
        gain_copy(r).start()

    @pl.when(sec % 2 == 1)
    def _():
        mate_copy.start()

    positions = lax.broadcasted_iota(jnp.int32, (1, blocks * BLOCK), 1)
    start = jnp.int32(0)
    slot = jnp.zeros_like(positions)
    source = jnp.zeros_like(positions)
    for j in range(slots):
        here = positions >= start
        slot = jnp.where(here, j, slot)
        source = jnp.where(here, ids_ref[j] * pool_ref.shape[1] - start + positions, source)
        start = start + len_ref[j]
    first_segments = seg_ref[pl.ds(sec, 1), :]
    prior_segments = seg_ref[pl.ds(jnp.maximum(sec - 1, 0), 1), :]
    second_segments = jnp.where(sec == 0, slot, prior_segments)
    for k in range(blocks):
        part = slice(k * BLOCK, (k + 1) * BLOCK)
        seg_rows[k] = first_segments[:, part]
        seg_rows[blocks + k] = second_segments[:, part]
        src_rows[k] = source[:, part] - sec * hosts_rows
    keys[...] = jnp.zeros_like(keys)
    values[...] = jnp.zeros_like(values)

    def picked(k):
        index = lax.broadcasted_iota(jnp.int32, (2 * hosts_rows, BLOCK), 0)
        hit = (index == src_rows[k]).astype(jnp.float32).astype(jnp.bfloat16)
        rows = pool_rows[...].reshape(2 * hosts_rows, cols)
        return lax.dot_general(
            hit, rows, (((0,), (0,)), ((), ())), preferred_element_type=jnp.float32
        )

    def pass_down(k):
        sum_copy(k).wait_recv()
        below[k] = (picked(k) + above[k].astype(jnp.float32)).astype(jnp.bfloat16)
        sum_copy(k).start()

    middle = even & (sec > 0) & (sec < top)

    @pl.when(even)
    def _():
        pool_copy.wait()
        mate_copy.wait_recv()

        @pl.when(sec == top)
        def _():
            def send(k, carry):
                below[k] = picked(k).astype(jnp.bfloat16)
                sum_copy(k).start()
                return carry

            lax.fori_loop(0, blocks, send, 0)

    for r in range(4):
        wkv_copies[r].wait()
        weight[r * cols:(r + 1) * cols, cols:] = kv_raw[r].T

    @pl.when(middle)
    def _():
        pass_down(0)

    late = jnp.minimum((top - sec) // 2, 2) - 1

    for copy in wq_copies:
        copy.wait()
    for r in (1, 2, 3):
        gain_copy(r).wait_recv()

    def forward(b):
        for way in range(2):
            own_copy(got.at[b, 0], b, way).wait_recv()
            forward_copy(b, way).start()

    forward(0)

    def step(b, carry):
        ahead = b + 2

        @pl.when(ahead < blocks)
        def _():
            for way in range(2):
                own_copy(
                    a_ref.at[0, pl.ds(pl.multiple_of(ahead * BLOCK, BLOCK), BLOCK)], ahead, way
                ).start()

        @pl.when((ahead >= blocks) & (ahead < steps))
        def _():
            k = ahead - blocks

            @pl.when(sec > 0)
            def _():
                hand_copy(k).wait_recv()

            @pl.when(sec == 0)
            def _():
                sum_copy(k).wait_recv()
                got[ahead, 0] = (picked(k) + above[k].astype(jnp.float32)).astype(jnp.bfloat16)

            for way in range(2):
                own_copy(got.at[ahead, 0], ahead, way).start()

        @pl.when(b + 1 < steps)
        def _():
            forward(b + 1)

        for way in range(2):
            forward_copy(b, way).wait_recv()

        @pl.when(b < blocks)
        def _():
            pltpu.make_async_copy(
                a_ref.at[0, pl.ds(0, BLOCK)], got.at[b, 0], x_sem.at[b]
            ).wait()

        total = jnp.zeros((BLOCK, 1), jnp.float32)
        for r in range(4):
            wide = got[b, r].astype(jnp.float32)
            total = total + jnp.sum(wide * wide, axis=1, keepdims=True)
        scale = lax.rsqrt(total / D + norm_eps)
        for r in range(4):
            wide = got[b, r].astype(jnp.float32)
            gain_row = gains[r].astype(jnp.float32)[0:1]
            normed[:, r * cols:(r + 1) * cols] = (wide * scale * gain_row).astype(jnp.bfloat16)

        def project(low, width):
            return jnp.dot(
                normed[...], weight[:, low:low + width], preferred_element_type=jnp.float32
            ).astype(jnp.bfloat16)

        keys[0:BLOCK] = keys[BLOCK:]
        values[0:BLOCK] = values[BLOCK:]
        keyval = project(cols, 2 * HEAD_DIM)
        keys[BLOCK:] = keyval[:, :HEAD_DIM]
        values[BLOCK:] = keyval[:, HEAD_DIM:]
        for low in range(0, cols, 256):
            query[:, low:low + 256] = project(low, 256)

        seg_here = seg_rows[b]
        seg_before = jnp.where(b % blocks > 0, seg_rows[jnp.maximum(b - 1, 0)], -1)
        seg_down = jnp.broadcast_to(seg_here, (BLOCK, BLOCK)).T
        row = lax.broadcasted_iota(jnp.int32, (BLOCK, BLOCK), 0)
        col = lax.broadcasted_iota(jnp.int32, (BLOCK, BLOCK), 1)
        allowed = jnp.concatenate(
            [
                jnp.where(seg_down == seg_before, 1, 0),
                jnp.where((seg_down == seg_here) & (col <= row), 1, 0),
            ],
            axis=1,
        ) > 0
        all_keys = keys[...]
        all_values = values[...]
        for h in range(cols // HEAD_DIM):
            part = slice(h * HEAD_DIM, (h + 1) * HEAD_DIM)
            scores = lax.dot_general(
                query[:, part], all_keys, (((1,), (1,)), ((), ())),
                preferred_element_type=jnp.float32,
            ) * HEAD_DIM ** (-0.5)
            scores = jnp.where(allowed, scores, masked_score)
            powers = jnp.exp(scores - jnp.max(scores, axis=1, keepdims=True))
            bottom = jnp.sum(powers, axis=1, keepdims=True)
            context = jnp.dot(
                powers.astype(jnp.bfloat16), all_values, preferred_element_type=jnp.float32
            ) / bottom
            context = context.astype(jnp.bfloat16).astype(jnp.float32)
            result[b, :, part] = (got[b, 0, :, part].astype(jnp.float32) + context).astype(
                jnp.bfloat16
            )

        rows = pl.ds(pl.multiple_of((b % blocks) * BLOCK, BLOCK), BLOCK)

        @pl.when(b < blocks)
        def _():
            @pl.when(sec < sections - 1)
            def _():
                hand_copy(b).start()

            pltpu.make_async_copy(result.at[b], out1_ref.at[0, rows], out_sem.at[b]).start()

        @pl.when(b >= blocks)
        def _():
            pltpu.make_async_copy(result.at[b], out2_ref.at[0, rows], out_sem.at[b]).start()

        down = b + 1 - late

        @pl.when(middle & (down >= 1) & (down < blocks))
        def _():
            pass_down(down)

        return carry

    lax.fori_loop(0, steps, step, 0)

    def drain(b, carry):
        for way in range(2):
            own_copy(got.at[b, 0], b, way).wait_send()
            forward_copy(b, way).wait_send()
        pltpu.make_async_copy(result.at[b], out1_ref.at[0, pl.ds(0, BLOCK)], out_sem.at[b]).wait()

        @pl.when(b < blocks)
        def _():
            @pl.when(sec < sections - 1)
            def _():
                hand_copy(b).wait_send()

            @pl.when(even & (sec > 0))
            def _():
                sum_copy(b).wait_send()

        return carry

    lax.fori_loop(0, steps, drain, 0)
    for r in (1, 2, 3):
        gain_copy(r).wait_send()

    @pl.when(sec % 2 == 1)
    def _():
        mate_copy.wait_send()


def relay(sections, activations, gain, w_query, w_kv, segments, pool, row_ids, row_lengths):
    tokens, cols = activations.shape[1:]
    blocks = tokens // BLOCK
    steps = 2 * blocks
    hosts_rows = pool.shape[0] * pool.shape[1]
    dma = pltpu.SemaphoreType.DMA
    bf16 = jnp.bfloat16
    anywhere = pl.BlockSpec(memory_space=pl.ANY)
    vmem = pl.BlockSpec(memory_space=pltpu.VMEM)
    smem = pl.BlockSpec(memory_space=pltpu.SMEM)
    return pl.pallas_call(
        functools.partial(relay_kernel, sections, hosts_rows, row_ids.shape[0]),
        out_shape=(
            jax.ShapeDtypeStruct(activations.shape, bf16),
            jax.ShapeDtypeStruct(activations.shape, bf16),
        ),
        in_specs=[anywhere, vmem, anywhere, anywhere, vmem, anywhere, smem, smem],
        out_specs=(anywhere, anywhere),
        scratch_shapes=[
            pltpu.VMEM((steps, 4, BLOCK, cols), bf16),
            pltpu.VMEM((4 * cols, cols + 2 * HEAD_DIM), bf16),
            pltpu.VMEM((4, 2 * HEAD_DIM, cols), bf16),
            pltpu.VMEM((4, 16, cols), bf16),
            pltpu.VMEM((BLOCK, 4 * cols), bf16),
            pltpu.VMEM((BLOCK, cols), bf16),
            pltpu.VMEM((2 * BLOCK, HEAD_DIM), bf16),
            pltpu.VMEM((2 * BLOCK, HEAD_DIM), bf16),
            pltpu.VMEM((steps, 1, BLOCK), jnp.int32),
            pltpu.VMEM((blocks, 1, BLOCK), jnp.int32),
            pltpu.VMEM((2, *pool.shape), bf16),
            pltpu.VMEM((blocks, BLOCK, cols), bf16),
            pltpu.VMEM((blocks, BLOCK, cols), bf16),
            pltpu.VMEM((steps, BLOCK, cols), bf16),
            dma((steps, 2)), dma((steps, 2)), dma((steps, 2)), dma((steps, 2)),
            dma((3,)), dma((3,)), dma((blocks,)), dma((blocks,)),
            dma((blocks,)), dma((4,)), dma((4,)), dma, dma, dma,
            dma((blocks,)), dma((blocks,)), dma((steps,)),
        ],
        compiler_params=pltpu.CompilerParams(
            collective_id=0, has_side_effects=True, vmem_limit_bytes=48 * 1024 * 1024
        ),
    )(activations, gain, w_query, w_kv, segments, pool, row_ids, row_lengths)


def solution(mesh):
    square = (
        mesh.shape["tensor"] == KV_HEADS == 4
        and mesh.shape["section"] % 2 == 0
        and mesh.shape["section"] >= 4
    )
    body = functools.partial(relay, mesh.shape["section"]) if square else per_device
    return jax.shard_map(
        body,
        mesh=mesh,
        in_specs=(
            P("section", None, "tensor"),
            P("section", "tensor"),
            P("section", None, "tensor"),
            P("section", "tensor", None),
            P(),
            P("section", None, "tensor"),
            P(),
            P(),
        ),
        out_specs=(P("section", None, "tensor"), P("section", None, "tensor")),
        check_vma=False,
    )
```

```python
import functools

import jax
import jax.numpy as jnp
from jax import lax
from jax.experimental import pallas as pl
from jax.experimental.pallas import tpu as pltpu
from jax.sharding import PartitionSpec as P

D = 4096
HEADS = 32
KV_HEADS = 4
HEAD_DIM = 128


norm_eps = 1e-05
masked_score = -1e30


def partner_2(block, axis, distance):
    count = lax.axis_size(axis)
    route = []
    for low in range(count):
        high = low | 1 << distance
        if high != low and high < count:
            route += [(low, high), (high, low)]
    return lax.ppermute(block, axis, route)


def from_behind(block, axis, distance):
    devices = range(lax.axis_size(axis))
    route = [(i - distance, i) for i in devices if i - distance in devices]
    return lax.ppermute(block, axis, route)


def attend(inputs, gain_cols, query_weight, keyval_weight, seg_ids, tensor_index):
    row_count, col_count = inputs.shape
    wide_inputs = inputs.astype(jnp.float32)
    square_total = lax.psum(jnp.sum(wide_inputs * wide_inputs, axis=1), "tensor")
    row_scale = lax.rsqrt(square_total / D + norm_eps)
    normed = (wide_inputs * row_scale[:, None] * gain_cols.astype(jnp.float32)[None, :]).astype(
        jnp.bfloat16
    )
    part_cols = lax.all_gather(normed, "tensor", axis=1, tiled=True)
    query_part = jnp.dot(part_cols, query_weight, preferred_element_type=jnp.float32)
    keyval_part = lax.dot_general(
        keyval_weight, part_cols, (((1,), (1,)), ((), ())), preferred_element_type=jnp.float32
    )
    query = query_part.astype(jnp.bfloat16)
    keyval = keyval_part.astype(jnp.bfloat16)
    heads_here = query_weight.shape[1] // HEAD_DIM
    group_size = HEADS // KV_HEADS
    group_devices = group_size // heads_here
    head_block = keyval
    for bit_number in range(group_devices.bit_length() - 1):
        partner = partner_2(head_block, "tensor", bit_number)
        is_lower = tensor_index // (1 << bit_number) % 2 == 0
        head_block = jnp.where(
            is_lower,
            jnp.concatenate([head_block, partner], axis=0),
            jnp.concatenate([partner, head_block], axis=0),
        )
    keys_cols = head_block[:HEAD_DIM]
    values_cols = head_block[HEAD_DIM:]
    query_heads = query.reshape(row_count, heads_here, HEAD_DIM)
    scores = jnp.einsum(
        "rhd,ds->hrs", query_heads, keys_cols, preferred_element_type=jnp.float32
    ) * HEAD_DIM ** (-0.5)
    positions = jnp.arange(row_count, dtype=jnp.int32)
    allowed = (seg_ids[:, None] == seg_ids[None, :]) & (positions[None, :] <= positions[:, None])
    scores = jnp.where(allowed[None, :, :], scores, masked_score)
    weights = jax.nn.softmax(scores, axis=-1).astype(jnp.bfloat16)
    context = jnp.einsum("hrs,ds->rhd", weights, values_cols, preferred_element_type=jnp.float32)
    context = context.astype(jnp.bfloat16).reshape(row_count, col_count)
    return (wide_inputs + context.astype(jnp.float32)).astype(jnp.bfloat16)


def pick_rows(running, host_rows, source):
    flat_rows = host_rows.reshape(-1, host_rows.shape[2])
    inside = (source >= 0) & (source < flat_rows.shape[0])
    taken = jnp.take(flat_rows, jnp.clip(source, 0, flat_rows.shape[0] - 1), axis=0)
    return jnp.where(inside[:, None], taken, running)


def per_device(activations, gain, w_query, w_kv, segments, pool, row_ids, row_lengths):
    section_index = lax.axis_index("section")
    tensor_index = lax.axis_index("tensor")
    token_count = activations.shape[1]
    col_count = activations.shape[2]
    own_segments = lax.dynamic_index_in_dim(segments, section_index, 0, keepdims=False)
    after_first = attend(activations[0], gain[0], w_query[0], w_kv[0], own_segments, tensor_index)[
        None
    ]
    ends = jnp.cumsum(row_lengths)
    positions = jnp.arange(token_count, dtype=jnp.int32)
    slot = jnp.sum((positions[:, None] >= ends[None, :]).astype(jnp.int32), axis=1)
    slot_match = slot[:, None] == jnp.arange(row_ids.shape[0], dtype=jnp.int32)[None, :]
    slot_start = jnp.sum(jnp.where(slot_match, (ends - row_lengths)[None, :], 0), axis=1)
    slot_row = jnp.sum(jnp.where(slot_match, row_ids[None, :], 0), axis=1)
    source = slot_row * pool.shape[1] + positions - slot_start
    empty_rows = jnp.zeros((token_count, col_count), jnp.bfloat16)
    fresh = pick_rows(empty_rows, lax.all_gather(pool, "section", axis=0, tiled=True), source)
    handed = from_behind(after_first, "section", 1)
    second_inputs = jnp.where(section_index == 0, fresh[None], handed)
    prior_segments = lax.dynamic_index_in_dim(
        segments, jnp.maximum(section_index - 1, 0), 0, keepdims=False
    )
    second_segments = jnp.where(section_index == 0, slot, prior_segments)
    after_second = attend(
        second_inputs[0], gain[0], w_query[0], w_kv[0], second_segments, tensor_index
    )[None]
    return (after_first, after_second)


BLOCK = 128
AT_ONCE = 4
LOG2_E = 1.4426950408889634
MESH = pl.DeviceIdType.MESH


def relay_kernel(
    sections, hosts_rows, slots,
    a_ref, gain_ref, wq_ref, wkv_ref, seg_ref, pool_ref, ids_ref, len_ref,
    out1_ref, out2_ref,
    got, weight, kv_raw, gains, normed, early, squares, query, keys, values, seg_rows, src_rows,
    pool_rows, above, below, result,
    own_send, own_recv, fwd_send, fwd_recv, gain_send, gain_recv, hand_send, hand_recv,
    x_sem, wq_sem, wkv_sem, pool_sem, mate_send, mate_recv, sum_send, sum_recv, out_sem,
):
    sec = lax.axis_index("section")
    ten = lax.axis_index("tensor")
    blocks = a_ref.shape[1] // BLOCK
    steps = 2 * blocks
    cols = a_ref.shape[2]
    over_x = ten + 1 - 2 * (ten % 2)
    over_y = ten + 2 - 4 * (ten // 2)
    peers = (ten, over_x, over_y, 3 - ten)
    even = sec % 2 == 0
    top = sections - 2

    x_copies = [
        pltpu.make_async_copy(
            a_ref.at[0, pl.ds(k * BLOCK, BLOCK)], got.at[k, 0], x_sem.at[k]
        )
        for k in range(blocks)
    ]
    wq_copies, wkv_copies = [], []
    for r in range(4):
        part = pl.ds(pl.multiple_of(peers[r] * cols, cols), cols)
        wq_copies.append(
            pltpu.make_async_copy(
                wq_ref.at[0, part], weight.at[pl.ds(r * cols, cols), pl.ds(0, cols)], wq_sem.at[r]
            )
        )
        wkv_copies.append(
            pltpu.make_async_copy(wkv_ref.at[0, :, part], kv_raw.at[r], wkv_sem.at[r])
        )
    pool_copy = pltpu.make_async_copy(pool_ref, pool_rows.at[0], pool_sem)
    x_copies[0].start()
    for copy in wkv_copies + wq_copies + x_copies[1:]:
        copy.start()

    @pl.when(even)
    def _():
        pool_copy.start()

    barrier = pltpu.get_barrier_semaphore()
    for r in (1, 2, 3):
        pl.semaphore_signal(barrier, inc=1, device_id=(sec, peers[r]), device_id_type=MESH)

    def greet(condition, other):
        @pl.when(condition)
        def _():
            pl.semaphore_signal(barrier, inc=1, device_id=(other, ten), device_id_type=MESH)

    greet(sec > 0, sec - 1)
    greet(sec < sections - 1, sec + 1)
    greet(even & (sec > 1), sec - 2)
    greet(even & (sec < top), sec + 2)
    others = 3
    for condition in (sec > 0, sec < sections - 1, even & (sec > 1), even & (sec < top)):
        others = others + jnp.where(condition, 1, 0)
    pl.semaphore_wait(barrier, others)

    def remote(src, dst, send_sem, recv_sem, device):
        return pltpu.make_async_remote_copy(
            src_ref=src, dst_ref=dst, send_sem=send_sem, recv_sem=recv_sem,
            device_id=device, device_id_type=MESH,
        )

    def own_copy(src, b, way):
        return remote(
            src, got.at[b, 1 + way], own_send.at[b, way], own_recv.at[b, way],
            (sec, peers[1 + way]),
        )

    half = BLOCK // 2

    def forward_copy(b, way):
        rows = pl.ds(way * half, half)
        return remote(
            got.at[b, 1 + way, rows], got.at[b, 3, rows], fwd_send.at[b, way],
            fwd_recv.at[b, way], (sec, peers[2 - way]),
        )

    def hand_copy(k):
        return remote(
            result.at[k], got.at[blocks + k, 0], hand_send.at[k], hand_recv.at[k], (sec + 1, ten)
        )

    def sum_copy(k):
        return remote(below.at[k], above.at[k], sum_send.at[k], sum_recv.at[k], (sec - 2, ten))

    def gain_copy(r):
        return remote(
            gains.at[0], gains.at[r], gain_send.at[r - 1], gain_recv.at[r - 1], (sec, peers[r])
        )

    mate_copy = remote(pool_ref, pool_rows.at[1], mate_send, mate_recv, (sec - 1, ten))

    for k in range(2):
        for way in range(2):
            own_copy(a_ref.at[0, pl.ds(k * BLOCK, BLOCK)], k, way).start()
    gains[0] = jnp.broadcast_to(gain_ref[...], gains.shape[1:])
    for r in (1, 2, 3):
        gain_copy(r).start()

    @pl.when(sec % 2 == 1)
    def _():
        mate_copy.start()

    positions = lax.broadcasted_iota(jnp.int32, (1, blocks * BLOCK), 1)
    start = jnp.int32(0)
    slot = jnp.zeros_like(positions)
    source = jnp.zeros_like(positions)
    for j in range(slots):
        here = positions >= start
        slot = jnp.where(here, j, slot)
        source = jnp.where(here, ids_ref[j] * pool_ref.shape[1] - start + positions, source)
        start = start + len_ref[j]
    first_segments = seg_ref[pl.ds(sec, 1), :]
    prior_segments = seg_ref[pl.ds(jnp.maximum(sec - 1, 0), 1), :]
    second_segments = jnp.where(sec == 0, slot, prior_segments)
    for k in range(blocks):
        part = slice(k * BLOCK, (k + 1) * BLOCK)
        seg_rows[k] = first_segments[:, part]
        seg_rows[blocks + k] = second_segments[:, part]
        src_rows[k] = source[:, part] - sec * hosts_rows
    keys[...] = jnp.zeros_like(keys)
    values[...] = jnp.zeros_like(values)

    def picked(k):
        index = lax.broadcasted_iota(jnp.int32, (2 * hosts_rows, BLOCK), 0)
        hit = (index == src_rows[k]).astype(jnp.float32).astype(jnp.bfloat16)
        rows = pool_rows[...].reshape(2 * hosts_rows, cols)
        return lax.dot_general(
            hit, rows, (((0,), (0,)), ((), ())), preferred_element_type=jnp.float32
        )

    def pass_down(k):
        sum_copy(k).wait_recv()
        below[k] = (picked(k) + above[k].astype(jnp.float32)).astype(jnp.bfloat16)
        sum_copy(k).start()

    middle = even & (sec > 0) & (sec < top)

    @pl.when(even)
    def _():
        pool_copy.wait()
        mate_copy.wait_recv()

        @pl.when(sec == top)
        def _():
            def send(k, carry):
                below[k] = picked(k).astype(jnp.bfloat16)
                sum_copy(k).start()
                return carry

            lax.fori_loop(0, blocks, send, 0)

    for r in range(4):
        wkv_copies[r].wait()
        weight[r * cols:(r + 1) * cols, cols:] = kv_raw[r].T

    @pl.when(middle)
    def _():
        pass_down(0)

    late = jnp.minimum((top - sec) // 2, 2) - 1

    for copy in wq_copies:
        copy.wait()
    for r in (1, 2, 3):
        gain_copy(r).wait_recv()

    def forward(b):
        for way in range(2):
            own_copy(got.at[b, 0], b, way).wait_recv()
            forward_copy(b, way).start()

    def scaled(b, r):
        wide = got[b, r].astype(jnp.float32)
        gain_row = gains[r].astype(jnp.float32)[0:1]
        normed[:, r * cols:(r + 1) * cols] = (wide * gain_row).astype(jnp.bfloat16)
        return jnp.sum(wide * wide, axis=1, keepdims=True)

    def begin(b):
        @pl.when(b < blocks)
        def _():
            pltpu.make_async_copy(
                a_ref.at[0, pl.ds(0, BLOCK)], got.at[b, 0], x_sem.at[b]
            ).wait()

        squares[...] = scaled(b, 0) + scaled(b, 1) + scaled(b, 2)
        for low in range(0, cols + 2 * HEAD_DIM, 256):
            early[:, low:low + 256] = jnp.dot(
                normed[:, :3 * cols], weight[:3 * cols, low:low + 256],
                preferred_element_type=jnp.float32,
            )

    forward(0)
    begin(0)

    def step(b, carry):
        ahead = b + 2

        @pl.when(ahead < blocks)
        def _():
            for way in range(2):
                own_copy(
                    a_ref.at[0, pl.ds(pl.multiple_of(ahead * BLOCK, BLOCK), BLOCK)], ahead, way
                ).start()

        @pl.when((ahead >= blocks) & (ahead < steps))
        def _():
            k = ahead - blocks

            @pl.when(sec > 0)
            def _():
                hand_copy(k).wait_recv()

            @pl.when(sec == 0)
            def _():
                sum_copy(k).wait_recv()
                got[ahead, 0] = (picked(k) + above[k].astype(jnp.float32)).astype(jnp.bfloat16)

            for way in range(2):
                own_copy(got.at[ahead, 0], ahead, way).start()

        @pl.when(b + 1 < steps)
        def _():
            forward(b + 1)

        for way in range(2):
            forward_copy(b, way).wait_recv()
        diagonal = scaled(b, 3)
        scale = lax.rsqrt((squares[...] + diagonal) / D + norm_eps)

        def project(low):
            late_part = jnp.dot(
                normed[:, 3 * cols:], weight[3 * cols:, low:low + 256],
                preferred_element_type=jnp.float32,
            )
            return ((early[:, low:low + 256] + late_part) * scale).astype(jnp.bfloat16)

        keys[0:BLOCK] = keys[BLOCK:]
        values[0:BLOCK] = values[BLOCK:]
        keyval = project(cols)
        keys[BLOCK:] = keyval[:, :HEAD_DIM]
        values[BLOCK:] = keyval[:, HEAD_DIM:]
        for low in range(0, cols, 256):
            two = project(low)
            query[low // HEAD_DIM] = two[:, :HEAD_DIM]
            query[low // HEAD_DIM + 1] = two[:, HEAD_DIM:]

        seg_here = seg_rows[b]
        seg_before = jnp.where(b % blocks > 0, seg_rows[jnp.maximum(b - 1, 0)], -1)
        seg_down = jnp.broadcast_to(seg_here, (BLOCK, BLOCK)).T
        row = lax.broadcasted_iota(jnp.int32, (BLOCK, BLOCK), 0)
        col = lax.broadcasted_iota(jnp.int32, (BLOCK, BLOCK), 1)
        allowed = jnp.concatenate(
            [
                jnp.where(seg_down == seg_before, 1, 0),
                jnp.where((seg_down == seg_here) & (col <= row), 1, 0),
            ],
            axis=1,
        )
        allowed = (allowed > 0)[None]
        all_keys = keys[...]
        all_values = values[...]
        for low in range(0, cols // HEAD_DIM, AT_ONCE):
            scores = lax.dot_general(
                query[low:low + AT_ONCE].reshape(AT_ONCE * BLOCK, HEAD_DIM), all_keys,
                (((1,), (1,)), ((), ())), preferred_element_type=jnp.float32,
            ).reshape(AT_ONCE, BLOCK, 2 * BLOCK) * (HEAD_DIM ** (-0.5) * LOG2_E)
            scores = jnp.where(allowed, scores, masked_score)
            powers = jnp.exp2(scores - jnp.max(scores, axis=2, keepdims=True))
            bottom = jnp.sum(powers, axis=2, keepdims=True)
            context = jnp.dot(
                powers.astype(jnp.bfloat16).reshape(AT_ONCE * BLOCK, 2 * BLOCK), all_values,
                preferred_element_type=jnp.float32,
            ).reshape(AT_ONCE, BLOCK, HEAD_DIM) / bottom
            context = context.astype(jnp.bfloat16).astype(jnp.float32)
            for h in range(AT_ONCE):
                part = slice((low + h) * HEAD_DIM, (low + h + 1) * HEAD_DIM)
                result[b, :, part] = (
                    got[b, 0, :, part].astype(jnp.float32) + context[h]
                ).astype(jnp.bfloat16)

        rows = pl.ds(pl.multiple_of((b % blocks) * BLOCK, BLOCK), BLOCK)

        @pl.when(b < blocks)
        def _():
            @pl.when(sec < sections - 1)
            def _():
                hand_copy(b).start()

            pltpu.make_async_copy(result.at[b], out1_ref.at[0, rows], out_sem.at[b]).start()

        @pl.when(b >= blocks)
        def _():
            pltpu.make_async_copy(result.at[b], out2_ref.at[0, rows], out_sem.at[b]).start()

        down = b + 1 - late

        @pl.when(middle & (down >= 1) & (down < blocks))
        def _():
            pass_down(down)

        @pl.when(b + 1 < steps)
        def _():
            begin(b + 1)

        return carry

    lax.fori_loop(0, steps, step, 0)

    def drain(b, carry):
        for way in range(2):
            own_copy(got.at[b, 0], b, way).wait_send()
            forward_copy(b, way).wait_send()
        pltpu.make_async_copy(result.at[b], out1_ref.at[0, pl.ds(0, BLOCK)], out_sem.at[b]).wait()

        @pl.when(b < blocks)
        def _():
            @pl.when(sec < sections - 1)
            def _():
                hand_copy(b).wait_send()

            @pl.when(even & (sec > 0))
            def _():
                sum_copy(b).wait_send()

        return carry

    lax.fori_loop(0, steps, drain, 0)
    for r in (1, 2, 3):
        gain_copy(r).wait_send()

    @pl.when(sec % 2 == 1)
    def _():
        mate_copy.wait_send()


def relay(sections, activations, gain, w_query, w_kv, segments, pool, row_ids, row_lengths):
    tokens, cols = activations.shape[1:]
    blocks = tokens // BLOCK
    steps = 2 * blocks
    hosts_rows = pool.shape[0] * pool.shape[1]
    dma = pltpu.SemaphoreType.DMA
    bf16 = jnp.bfloat16
    anywhere = pl.BlockSpec(memory_space=pl.ANY)
    vmem = pl.BlockSpec(memory_space=pltpu.VMEM)
    smem = pl.BlockSpec(memory_space=pltpu.SMEM)
    return pl.pallas_call(
        functools.partial(relay_kernel, sections, hosts_rows, row_ids.shape[0]),
        out_shape=(
            jax.ShapeDtypeStruct(activations.shape, bf16),
            jax.ShapeDtypeStruct(activations.shape, bf16),
        ),
        in_specs=[anywhere, vmem, anywhere, anywhere, vmem, anywhere, smem, smem],
        out_specs=(anywhere, anywhere),
        scratch_shapes=[
            pltpu.VMEM((steps, 4, BLOCK, cols), bf16),
            pltpu.VMEM((4 * cols, cols + 2 * HEAD_DIM), bf16),
            pltpu.VMEM((4, 2 * HEAD_DIM, cols), bf16),
            pltpu.VMEM((4, 16, cols), bf16),
            pltpu.VMEM((BLOCK, 4 * cols), bf16),
            pltpu.VMEM((BLOCK, cols + 2 * HEAD_DIM), jnp.float32),
            pltpu.VMEM((BLOCK, 1), jnp.float32),
            pltpu.VMEM((cols // HEAD_DIM, BLOCK, HEAD_DIM), bf16),
            pltpu.VMEM((2 * BLOCK, HEAD_DIM), bf16),
            pltpu.VMEM((2 * BLOCK, HEAD_DIM), bf16),
            pltpu.VMEM((steps, 1, BLOCK), jnp.int32),
            pltpu.VMEM((blocks, 1, BLOCK), jnp.int32),
            pltpu.VMEM((2, *pool.shape), bf16),
            pltpu.VMEM((blocks, BLOCK, cols), bf16),
            pltpu.VMEM((blocks, BLOCK, cols), bf16),
            pltpu.VMEM((steps, BLOCK, cols), bf16),
            dma((steps, 2)), dma((steps, 2)), dma((steps, 2)), dma((steps, 2)),
            dma((3,)), dma((3,)), dma((blocks,)), dma((blocks,)),
            dma((blocks,)), dma((4,)), dma((4,)), dma, dma, dma,
            dma((blocks,)), dma((blocks,)), dma((steps,)),
        ],
        compiler_params=pltpu.CompilerParams(
            collective_id=0, has_side_effects=True, vmem_limit_bytes=63 * 1024 * 1024
        ),
    )(activations, gain, w_query, w_kv, segments, pool, row_ids, row_lengths)


def solution(mesh):
    square = (
        mesh.shape["tensor"] == KV_HEADS == 4
        and mesh.shape["section"] % 2 == 0
        and mesh.shape["section"] >= 4
    )
    body = functools.partial(relay, mesh.shape["section"]) if square else per_device
    return jax.shard_map(
        body,
        mesh=mesh,
        in_specs=(
            P("section", None, "tensor"),
            P("section", "tensor"),
            P("section", None, "tensor"),
            P("section", "tensor", None),
            P(),
            P("section", None, "tensor"),
            P(),
            P(),
        ),
        out_specs=(P("section", None, "tensor"), P("section", None, "tensor")),
        check_vma=False,
    )
```

```python
import functools

import jax
import jax.numpy as jnp
from jax import lax
from jax.experimental import pallas as pl
from jax.experimental.pallas import tpu as pltpu
from jax.sharding import PartitionSpec as P

D = 4096
HEADS = 32
KV_HEADS = 4
HEAD_DIM = 128


norm_eps = 1e-05
masked_score = -1e30


def partner_2(block, axis, distance):
    count = lax.axis_size(axis)
    route = []
    for low in range(count):
        high = low | 1 << distance
        if high != low and high < count:
            route += [(low, high), (high, low)]
    return lax.ppermute(block, axis, route)


def from_behind(block, axis, distance):
    devices = range(lax.axis_size(axis))
    route = [(i - distance, i) for i in devices if i - distance in devices]
    return lax.ppermute(block, axis, route)


def attend(inputs, gain_cols, query_weight, keyval_weight, seg_ids, tensor_index):
    row_count, col_count = inputs.shape
    wide_inputs = inputs.astype(jnp.float32)
    square_total = lax.psum(jnp.sum(wide_inputs * wide_inputs, axis=1), "tensor")
    row_scale = lax.rsqrt(square_total / D + norm_eps)
    normed = (wide_inputs * row_scale[:, None] * gain_cols.astype(jnp.float32)[None, :]).astype(
        jnp.bfloat16
    )
    part_cols = lax.all_gather(normed, "tensor", axis=1, tiled=True)
    query_part = jnp.dot(part_cols, query_weight, preferred_element_type=jnp.float32)
    keyval_part = lax.dot_general(
        keyval_weight, part_cols, (((1,), (1,)), ((), ())), preferred_element_type=jnp.float32
    )
    query = query_part.astype(jnp.bfloat16)
    keyval = keyval_part.astype(jnp.bfloat16)
    heads_here = query_weight.shape[1] // HEAD_DIM
    group_size = HEADS // KV_HEADS
    group_devices = group_size // heads_here
    head_block = keyval
    for bit_number in range(group_devices.bit_length() - 1):
        partner = partner_2(head_block, "tensor", bit_number)
        is_lower = tensor_index // (1 << bit_number) % 2 == 0
        head_block = jnp.where(
            is_lower,
            jnp.concatenate([head_block, partner], axis=0),
            jnp.concatenate([partner, head_block], axis=0),
        )
    keys_cols = head_block[:HEAD_DIM]
    values_cols = head_block[HEAD_DIM:]
    query_heads = query.reshape(row_count, heads_here, HEAD_DIM)
    scores = jnp.einsum(
        "rhd,ds->hrs", query_heads, keys_cols, preferred_element_type=jnp.float32
    ) * HEAD_DIM ** (-0.5)
    positions = jnp.arange(row_count, dtype=jnp.int32)
    allowed = (seg_ids[:, None] == seg_ids[None, :]) & (positions[None, :] <= positions[:, None])
    scores = jnp.where(allowed[None, :, :], scores, masked_score)
    weights = jax.nn.softmax(scores, axis=-1).astype(jnp.bfloat16)
    context = jnp.einsum("hrs,ds->rhd", weights, values_cols, preferred_element_type=jnp.float32)
    context = context.astype(jnp.bfloat16).reshape(row_count, col_count)
    return (wide_inputs + context.astype(jnp.float32)).astype(jnp.bfloat16)


def pick_rows(running, host_rows, source):
    flat_rows = host_rows.reshape(-1, host_rows.shape[2])
    inside = (source >= 0) & (source < flat_rows.shape[0])
    taken = jnp.take(flat_rows, jnp.clip(source, 0, flat_rows.shape[0] - 1), axis=0)
    return jnp.where(inside[:, None], taken, running)


def per_device(activations, gain, w_query, w_kv, segments, pool, row_ids, row_lengths):
    section_index = lax.axis_index("section")
    tensor_index = lax.axis_index("tensor")
    token_count = activations.shape[1]
    col_count = activations.shape[2]
    own_segments = lax.dynamic_index_in_dim(segments, section_index, 0, keepdims=False)
    after_first = attend(activations[0], gain[0], w_query[0], w_kv[0], own_segments, tensor_index)[
        None
    ]
    ends = jnp.cumsum(row_lengths)
    positions = jnp.arange(token_count, dtype=jnp.int32)
    slot = jnp.sum((positions[:, None] >= ends[None, :]).astype(jnp.int32), axis=1)
    slot_match = slot[:, None] == jnp.arange(row_ids.shape[0], dtype=jnp.int32)[None, :]
    slot_start = jnp.sum(jnp.where(slot_match, (ends - row_lengths)[None, :], 0), axis=1)
    slot_row = jnp.sum(jnp.where(slot_match, row_ids[None, :], 0), axis=1)
    source = slot_row * pool.shape[1] + positions - slot_start
    empty_rows = jnp.zeros((token_count, col_count), jnp.bfloat16)
    fresh = pick_rows(empty_rows, lax.all_gather(pool, "section", axis=0, tiled=True), source)
    handed = from_behind(after_first, "section", 1)
    second_inputs = jnp.where(section_index == 0, fresh[None], handed)
    prior_segments = lax.dynamic_index_in_dim(
        segments, jnp.maximum(section_index - 1, 0), 0, keepdims=False
    )
    second_segments = jnp.where(section_index == 0, slot, prior_segments)
    after_second = attend(
        second_inputs[0], gain[0], w_query[0], w_kv[0], second_segments, tensor_index
    )[None]
    return (after_first, after_second)


BLOCK = 128
AT_ONCE = 4
LOG2_E = 1.4426950408889634
MESH = pl.DeviceIdType.MESH


def relay_kernel(
    sections, hosts_rows, slots,
    a_ref, gain_hbm, wq_ref, wkv_ref, seg_hbm, pool_ref, ids_hbm, len_hbm,
    out1_ref, out2_ref,
    gain_ref, seg_ref, ids_ref, len_ref, small_sem, got, weight, kv_raw, gains, normed, early, squares, query, keys, values, seg_rows, src_rows,
    pool_rows, above, below, result,
    own_send, own_recv, fwd_send, fwd_recv, gain_send, gain_recv, hand_send, hand_recv,
    x_sem, wq_sem, wkv_sem, pool_sem, mate_send, mate_recv, sum_send, sum_recv, out_sem,
):
    sec = lax.axis_index("section")
    ten = lax.axis_index("tensor")
    blocks = a_ref.shape[1] // BLOCK
    steps = 2 * blocks
    cols = a_ref.shape[2]
    over_x = ten + 1 - 2 * (ten % 2)
    over_y = ten + 2 - 4 * (ten // 2)
    peers = (ten, over_x, over_y, 3 - ten)
    even = sec % 2 == 0
    top = sections - 2

    x_copies = [
        pltpu.make_async_copy(
            a_ref.at[0, pl.ds(k * BLOCK, BLOCK)], got.at[k, 0], x_sem.at[k]
        )
        for k in range(blocks)
    ]
    wq_copies, wkv_copies = [], []
    for r in range(4):
        part = pl.ds(pl.multiple_of(peers[r] * cols, cols), cols)
        wq_copies.append(
            pltpu.make_async_copy(
                wq_ref.at[0, part], weight.at[pl.ds(r * cols, cols), pl.ds(0, cols)], wq_sem.at[r]
            )
        )
        wkv_copies.append(
            pltpu.make_async_copy(wkv_ref.at[0, :, part], kv_raw.at[r], wkv_sem.at[r])
        )
    pool_copy = pltpu.make_async_copy(pool_ref, pool_rows.at[0], pool_sem)
    small_copies = [
        pltpu.make_async_copy(src, dst, small_sem.at[i])
        for i, (src, dst) in enumerate(
            ((gain_hbm, gain_ref), (seg_hbm, seg_ref), (ids_hbm, ids_ref), (len_hbm, len_ref))
        )
    ]
    for copy in small_copies:
        copy.start()

    barrier = pltpu.get_barrier_semaphore()
    for r in (1, 2, 3):
        pl.semaphore_signal(barrier, inc=1, device_id=(sec, peers[r]), device_id_type=MESH)

    def greet(condition, other):
        @pl.when(condition)
        def _():
            pl.semaphore_signal(barrier, inc=1, device_id=(other, ten), device_id_type=MESH)

    greet(sec > 0, sec - 1)
    greet(sec < sections - 1, sec + 1)
    greet(even & (sec > 1), sec - 2)
    greet(even & (sec < top), sec + 2)
    others = 3
    for condition in (sec > 0, sec < sections - 1, even & (sec > 1), even & (sec < top)):
        others = others + jnp.where(condition, 1, 0)
    pl.semaphore_wait(barrier, others)

    def remote(src, dst, send_sem, recv_sem, device):
        return pltpu.make_async_remote_copy(
            src_ref=src, dst_ref=dst, send_sem=send_sem, recv_sem=recv_sem,
            device_id=device, device_id_type=MESH,
        )

    def own_copy(src, b, way):
        return remote(
            src, got.at[b, 1 + way], own_send.at[b, way], own_recv.at[b, way],
            (sec, peers[1 + way]),
        )

    half = BLOCK // 2

    def forward_copy(b, way):
        rows = pl.ds(way * half, half)
        return remote(
            got.at[b, 1 + way, rows], got.at[b, 3, rows], fwd_send.at[b, way],
            fwd_recv.at[b, way], (sec, peers[2 - way]),
        )

    def hand_copy(k):
        return remote(
            result.at[k], got.at[blocks + k, 0], hand_send.at[k], hand_recv.at[k], (sec + 1, ten)
        )

    def sum_copy(k):
        return remote(below.at[k], above.at[k], sum_send.at[k], sum_recv.at[k], (sec - 2, ten))

    def gain_copy(r):
        return remote(
            gains.at[0], gains.at[r], gain_send.at[r - 1], gain_recv.at[r - 1], (sec, peers[r])
        )

    mate_copy = remote(pool_ref, pool_rows.at[1], mate_send, mate_recv, (sec - 1, ten))

    for k in range(3):
        for way in range(2):
            own_copy(a_ref.at[0, pl.ds(k * BLOCK, BLOCK)], k, way).start()
    for copy in wkv_copies + x_copies[:1] + wq_copies + x_copies[1:]:
        copy.start()

    @pl.when(even)
    def _():
        pool_copy.start()

    for copy in small_copies:
        copy.wait()
    gains[0] = jnp.broadcast_to(gain_ref[...], gains.shape[1:])
    for r in (1, 2, 3):
        gain_copy(r).start()

    @pl.when(sec % 2 == 1)
    def _():
        mate_copy.start()

    positions = lax.broadcasted_iota(jnp.int32, (1, blocks * BLOCK), 1)
    start = jnp.int32(0)
    slot = jnp.zeros_like(positions)
    source = jnp.zeros_like(positions)
    for j in range(slots):
        here = positions >= start
        slot = jnp.where(here, j, slot)
        source = jnp.where(here, ids_ref[j] * pool_ref.shape[1] - start + positions, source)
        start = start + len_ref[j]
    first_segments = seg_ref[pl.ds(sec, 1), :]
    prior_segments = seg_ref[pl.ds(jnp.maximum(sec - 1, 0), 1), :]
    second_segments = jnp.where(sec == 0, slot, prior_segments)
    for k in range(blocks):
        part = slice(k * BLOCK, (k + 1) * BLOCK)
        seg_rows[k] = first_segments[:, part]
        seg_rows[blocks + k] = second_segments[:, part]
        src_rows[k] = source[:, part] - sec * hosts_rows
    keys[...] = jnp.zeros_like(keys)
    values[...] = jnp.zeros_like(values)

    def picked(k):
        index = lax.broadcasted_iota(jnp.int32, (2 * hosts_rows, BLOCK), 0)
        hit = (index == src_rows[k]).astype(jnp.float32).astype(jnp.bfloat16)
        rows = pool_rows[...].reshape(2 * hosts_rows, cols)
        return lax.dot_general(
            hit, rows, (((0,), (0,)), ((), ())), preferred_element_type=jnp.float32
        )

    def pass_down(k):
        sum_copy(k).wait_recv()
        below[k] = (picked(k) + above[k].astype(jnp.float32)).astype(jnp.bfloat16)
        sum_copy(k).start()

    middle = even & (sec > 0) & (sec < top)

    @pl.when(even)
    def _():
        pool_copy.wait()
        mate_copy.wait_recv()

        @pl.when(sec == top)
        def _():
            def send(k, carry):
                below[k] = picked(k).astype(jnp.bfloat16)
                sum_copy(k).start()
                return carry

            lax.fori_loop(0, blocks, send, 0)

    for r in range(4):
        wkv_copies[r].wait()
        weight[r * cols:(r + 1) * cols, cols:] = kv_raw[r].T

    late = jnp.minimum((top - sec) // 2, 2) - 1

    for copy in wq_copies:
        copy.wait()
    for r in (1, 2, 3):
        gain_copy(r).wait_recv()

    def forward(b):
        for way in range(2):
            own_copy(got.at[b, 0], b, way).wait_recv()
            forward_copy(b, way).start()

    def scaled(b, r):
        wide = got[b, r].astype(jnp.float32)
        gain_row = gains[r].astype(jnp.float32)[0:1]
        normed[:, r * cols:(r + 1) * cols] = (wide * gain_row).astype(jnp.bfloat16)
        return jnp.sum(wide * wide, axis=1, keepdims=True)

    def begin(b):
        @pl.when(b < blocks)
        def _():
            pltpu.make_async_copy(
                a_ref.at[0, pl.ds(0, BLOCK)], got.at[b, 0], x_sem.at[b]
            ).wait()

        squares[...] = scaled(b, 0) + scaled(b, 1) + scaled(b, 2)
        for low in range(0, cols + 2 * HEAD_DIM, 256):
            early[:, low:low + 256] = jnp.dot(
                normed[:, :3 * cols], weight[:3 * cols, low:low + 256],
                preferred_element_type=jnp.float32,
            )

    forward(0)

    @pl.when(middle)
    def _():
        pass_down(0)

    begin(0)

    def step(b, carry):
        @pl.when(b + 1 < steps)
        def _():
            forward(b + 1)

        for way in range(2):
            forward_copy(b, way).wait_recv()
        diagonal = scaled(b, 3)
        scale = lax.rsqrt((squares[...] + diagonal) / D + norm_eps)

        def project(low):
            late_part = jnp.dot(
                normed[:, 3 * cols:], weight[3 * cols:, low:low + 256],
                preferred_element_type=jnp.float32,
            )
            return ((early[:, low:low + 256] + late_part) * scale).astype(jnp.bfloat16)

        keys[0:BLOCK] = keys[BLOCK:]
        values[0:BLOCK] = values[BLOCK:]
        keyval = project(cols)
        keys[BLOCK:] = keyval[:, :HEAD_DIM]
        values[BLOCK:] = keyval[:, HEAD_DIM:]
        for low in range(0, cols, 256):
            two = project(low)
            query[low // HEAD_DIM] = two[:, :HEAD_DIM]
            query[low // HEAD_DIM + 1] = two[:, HEAD_DIM:]

        seg_here = seg_rows[b]
        seg_before = jnp.where(b % blocks > 0, seg_rows[jnp.maximum(b - 1, 0)], -1)
        seg_down = jnp.broadcast_to(seg_here, (BLOCK, BLOCK)).T
        row = lax.broadcasted_iota(jnp.int32, (BLOCK, BLOCK), 0)
        col = lax.broadcasted_iota(jnp.int32, (BLOCK, BLOCK), 1)
        allowed = jnp.concatenate(
            [
                jnp.where(seg_down == seg_before, 1, 0),
                jnp.where((seg_down == seg_here) & (col <= row), 1, 0),
            ],
            axis=1,
        )
        allowed = (allowed > 0)[None]
        all_keys = keys[...]
        all_values = values[...]
        for low in range(0, cols // HEAD_DIM, AT_ONCE):
            scores = lax.dot_general(
                query[low:low + AT_ONCE].reshape(AT_ONCE * BLOCK, HEAD_DIM), all_keys,
                (((1,), (1,)), ((), ())), preferred_element_type=jnp.float32,
            ).reshape(AT_ONCE, BLOCK, 2 * BLOCK) * (HEAD_DIM ** (-0.5) * LOG2_E)
            scores = jnp.where(allowed, scores, masked_score)
            powers = jnp.exp2(scores - jnp.max(scores, axis=2, keepdims=True))
            bottom = jnp.sum(powers, axis=2, keepdims=True)
            context = jnp.dot(
                powers.astype(jnp.bfloat16).reshape(AT_ONCE * BLOCK, 2 * BLOCK), all_values,
                preferred_element_type=jnp.float32,
            ).reshape(AT_ONCE, BLOCK, HEAD_DIM) / bottom
            context = context.astype(jnp.bfloat16).astype(jnp.float32)
            for h in range(AT_ONCE):
                part = slice((low + h) * HEAD_DIM, (low + h + 1) * HEAD_DIM)
                result[b, :, part] = (
                    got[b, 0, :, part].astype(jnp.float32) + context[h]
                ).astype(jnp.bfloat16)

        rows = pl.ds(pl.multiple_of((b % blocks) * BLOCK, BLOCK), BLOCK)

        @pl.when(b < blocks)
        def _():
            @pl.when(sec < sections - 1)
            def _():
                hand_copy(b).start()

            pltpu.make_async_copy(result.at[b], out1_ref.at[0, rows], out_sem.at[b]).start()

        @pl.when(b >= blocks)
        def _():
            pltpu.make_async_copy(result.at[b], out2_ref.at[0, rows], out_sem.at[b]).start()

        ahead = b + 3

        @pl.when(ahead < blocks)
        def _():
            for way in range(2):
                own_copy(
                    a_ref.at[0, pl.ds(pl.multiple_of(ahead * BLOCK, BLOCK), BLOCK)], ahead, way
                ).start()

        @pl.when((ahead >= blocks) & (ahead < steps))
        def _():
            k = ahead - blocks

            @pl.when(sec > 0)
            def _():
                hand_copy(k).wait_recv()

            @pl.when(sec == 0)
            def _():
                sum_copy(k).wait_recv()
                got[ahead, 0] = (picked(k) + above[k].astype(jnp.float32)).astype(jnp.bfloat16)

            for way in range(2):
                own_copy(got.at[ahead, 0], ahead, way).start()

        down = b + 1 - late

        @pl.when(middle & (down >= 1) & (down < blocks))
        def _():
            pass_down(down)

        @pl.when(b + 1 < steps)
        def _():
            begin(b + 1)

        return carry

    lax.fori_loop(0, steps, step, 0)

    def drain(b, carry):
        for way in range(2):
            own_copy(got.at[b, 0], b, way).wait_send()
            forward_copy(b, way).wait_send()
        pltpu.make_async_copy(result.at[b], out1_ref.at[0, pl.ds(0, BLOCK)], out_sem.at[b]).wait()

        @pl.when(b < blocks)
        def _():
            @pl.when(sec < sections - 1)
            def _():
                hand_copy(b).wait_send()

            @pl.when(even & (sec > 0))
            def _():
                sum_copy(b).wait_send()

        return carry

    lax.fori_loop(0, steps, drain, 0)
    for r in (1, 2, 3):
        gain_copy(r).wait_send()

    @pl.when(sec % 2 == 1)
    def _():
        mate_copy.wait_send()


def relay(sections, activations, gain, w_query, w_kv, segments, pool, row_ids, row_lengths):
    tokens, cols = activations.shape[1:]
    blocks = tokens // BLOCK
    steps = 2 * blocks
    hosts_rows = pool.shape[0] * pool.shape[1]
    dma = pltpu.SemaphoreType.DMA
    bf16 = jnp.bfloat16
    anywhere = pl.BlockSpec(memory_space=pl.ANY)
    hbm = pl.BlockSpec(memory_space=pltpu.HBM)
    return pl.pallas_call(
        functools.partial(relay_kernel, sections, hosts_rows, row_ids.shape[0]),
        out_shape=(
            jax.ShapeDtypeStruct(activations.shape, bf16),
            jax.ShapeDtypeStruct(activations.shape, bf16),
        ),
        in_specs=[hbm] * 8,
        out_specs=(anywhere, anywhere),
        scratch_shapes=[
            pltpu.VMEM(gain.shape, bf16),
            pltpu.VMEM(segments.shape, jnp.int32),
            pltpu.SMEM(row_ids.shape, jnp.int32),
            pltpu.SMEM(row_lengths.shape, jnp.int32),
            dma((4,)),
            pltpu.VMEM((steps, 4, BLOCK, cols), bf16),
            pltpu.VMEM((4 * cols, cols + 2 * HEAD_DIM), bf16),
            pltpu.VMEM((4, 2 * HEAD_DIM, cols), bf16),
            pltpu.VMEM((4, 16, cols), bf16),
            pltpu.VMEM((BLOCK, 4 * cols), bf16),
            pltpu.VMEM((BLOCK, cols + 2 * HEAD_DIM), jnp.float32),
            pltpu.VMEM((BLOCK, 1), jnp.float32),
            pltpu.VMEM((cols // HEAD_DIM, BLOCK, HEAD_DIM), bf16),
            pltpu.VMEM((2 * BLOCK, HEAD_DIM), bf16),
            pltpu.VMEM((2 * BLOCK, HEAD_DIM), bf16),
            pltpu.VMEM((steps, 1, BLOCK), jnp.int32),
            pltpu.VMEM((blocks, 1, BLOCK), jnp.int32),
            pltpu.VMEM((2, *pool.shape), bf16),
            pltpu.VMEM((blocks, BLOCK, cols), bf16),
            pltpu.VMEM((blocks, BLOCK, cols), bf16),
            pltpu.VMEM((steps, BLOCK, cols), bf16),
            dma((steps, 2)), dma((steps, 2)), dma((steps, 2)), dma((steps, 2)),
            dma((3,)), dma((3,)), dma((blocks,)), dma((blocks,)),
            dma((blocks,)), dma((4,)), dma((4,)), dma, dma, dma,
            dma((blocks,)), dma((blocks,)), dma((steps,)),
        ],
        compiler_params=pltpu.CompilerParams(
            collective_id=0, has_side_effects=True, vmem_limit_bytes=48 * 1024 * 1024
        ),
    )(
        *(
            pltpu.with_memory_space_constraint(argument, pltpu.HBM)
            for argument in (
                activations, gain, w_query, w_kv, segments, pool, row_ids, row_lengths
            )
        )
    )


def solution(mesh):
    square = (
        mesh.shape["tensor"] == KV_HEADS == 4
        and mesh.shape["section"] % 2 == 0
        and mesh.shape["section"] >= 4
    )
    body = functools.partial(relay, mesh.shape["section"]) if square else per_device
    return jax.shard_map(
        body,
        mesh=mesh,
        in_specs=(
            P("section", None, "tensor"),
            P("section", "tensor"),
            P("section", None, "tensor"),
            P("section", "tensor", None),
            P(),
            P("section", None, "tensor"),
            P(),
            P(),
        ),
        out_specs=(P("section", None, "tensor"), P("section", None, "tensor")),
        check_vma=False,
    )
```

```python
import functools

import jax
import jax.numpy as jnp
from jax import lax
from jax.experimental import pallas as pl
from jax.experimental.pallas import tpu as pltpu
from jax.sharding import PartitionSpec as P

D = 4096
HEADS = 32
KV_HEADS = 4
HEAD_DIM = 128


norm_eps = 1e-05
masked_score = -1e30


def partner_2(block, axis, distance):
    count = lax.axis_size(axis)
    route = []
    for low in range(count):
        high = low | 1 << distance
        if high != low and high < count:
            route += [(low, high), (high, low)]
    return lax.ppermute(block, axis, route)


def from_behind(block, axis, distance):
    devices = range(lax.axis_size(axis))
    route = [(i - distance, i) for i in devices if i - distance in devices]
    return lax.ppermute(block, axis, route)


def attend(inputs, gain_cols, query_weight, keyval_weight, seg_ids, tensor_index):
    row_count, col_count = inputs.shape
    wide_inputs = inputs.astype(jnp.float32)
    square_total = lax.psum(jnp.sum(wide_inputs * wide_inputs, axis=1), "tensor")
    row_scale = lax.rsqrt(square_total / D + norm_eps)
    normed = (wide_inputs * row_scale[:, None] * gain_cols.astype(jnp.float32)[None, :]).astype(
        jnp.bfloat16
    )
    part_cols = lax.all_gather(normed, "tensor", axis=1, tiled=True)
    query_part = jnp.dot(part_cols, query_weight, preferred_element_type=jnp.float32)
    keyval_part = lax.dot_general(
        keyval_weight, part_cols, (((1,), (1,)), ((), ())), preferred_element_type=jnp.float32
    )
    query = query_part.astype(jnp.bfloat16)
    keyval = keyval_part.astype(jnp.bfloat16)
    heads_here = query_weight.shape[1] // HEAD_DIM
    group_size = HEADS // KV_HEADS
    group_devices = group_size // heads_here
    head_block = keyval
    for bit_number in range(group_devices.bit_length() - 1):
        partner = partner_2(head_block, "tensor", bit_number)
        is_lower = tensor_index // (1 << bit_number) % 2 == 0
        head_block = jnp.where(
            is_lower,
            jnp.concatenate([head_block, partner], axis=0),
            jnp.concatenate([partner, head_block], axis=0),
        )
    keys_cols = head_block[:HEAD_DIM]
    values_cols = head_block[HEAD_DIM:]
    query_heads = query.reshape(row_count, heads_here, HEAD_DIM)
    scores = jnp.einsum(
        "rhd,ds->hrs", query_heads, keys_cols, preferred_element_type=jnp.float32
    ) * HEAD_DIM ** (-0.5)
    positions = jnp.arange(row_count, dtype=jnp.int32)
    allowed = (seg_ids[:, None] == seg_ids[None, :]) & (positions[None, :] <= positions[:, None])
    scores = jnp.where(allowed[None, :, :], scores, masked_score)
    weights = jax.nn.softmax(scores, axis=-1).astype(jnp.bfloat16)
    context = jnp.einsum("hrs,ds->rhd", weights, values_cols, preferred_element_type=jnp.float32)
    context = context.astype(jnp.bfloat16).reshape(row_count, col_count)
    return (wide_inputs + context.astype(jnp.float32)).astype(jnp.bfloat16)


def pick_rows(running, host_rows, source):
    flat_rows = host_rows.reshape(-1, host_rows.shape[2])
    inside = (source >= 0) & (source < flat_rows.shape[0])
    taken = jnp.take(flat_rows, jnp.clip(source, 0, flat_rows.shape[0] - 1), axis=0)
    return jnp.where(inside[:, None], taken, running)


def per_device(activations, gain, w_query, w_kv, segments, pool, row_ids, row_lengths):
    section_index = lax.axis_index("section")
    tensor_index = lax.axis_index("tensor")
    token_count = activations.shape[1]
    col_count = activations.shape[2]
    own_segments = lax.dynamic_index_in_dim(segments, section_index, 0, keepdims=False)
    after_first = attend(activations[0], gain[0], w_query[0], w_kv[0], own_segments, tensor_index)[
        None
    ]
    ends = jnp.cumsum(row_lengths)
    positions = jnp.arange(token_count, dtype=jnp.int32)
    slot = jnp.sum((positions[:, None] >= ends[None, :]).astype(jnp.int32), axis=1)
    slot_match = slot[:, None] == jnp.arange(row_ids.shape[0], dtype=jnp.int32)[None, :]
    slot_start = jnp.sum(jnp.where(slot_match, (ends - row_lengths)[None, :], 0), axis=1)
    slot_row = jnp.sum(jnp.where(slot_match, row_ids[None, :], 0), axis=1)
    source = slot_row * pool.shape[1] + positions - slot_start
    empty_rows = jnp.zeros((token_count, col_count), jnp.bfloat16)
    fresh = pick_rows(empty_rows, lax.all_gather(pool, "section", axis=0, tiled=True), source)
    handed = from_behind(after_first, "section", 1)
    second_inputs = jnp.where(section_index == 0, fresh[None], handed)
    prior_segments = lax.dynamic_index_in_dim(
        segments, jnp.maximum(section_index - 1, 0), 0, keepdims=False
    )
    second_segments = jnp.where(section_index == 0, slot, prior_segments)
    after_second = attend(
        second_inputs[0], gain[0], w_query[0], w_kv[0], second_segments, tensor_index
    )[None]
    return (after_first, after_second)


BLOCK = 128
AT_ONCE = 4
LOG2_E = 1.4426950408889634
MESH = pl.DeviceIdType.MESH


def relay_kernel(
    sections, hosts_rows, slots,
    a_ref, gain_hbm, wq_ref, wkv_ref, seg_hbm, pool_ref, ids_hbm, len_hbm,
    out1_ref, out2_ref,
    gain_ref, seg_ref, ids_ref, len_ref, small_sem, got, weight, kv_raw, gains, normed, early, squares, query, keys, values, seg_rows, src_rows,
    pool_rows, above, below, result,
    own_send, own_recv, fwd_send, fwd_recv, gain_send, gain_recv, hand_send, hand_recv,
    x_sem, wq_sem, wkv_sem, pool_sem, mate_send, mate_recv, sum_send, sum_recv, out_sem,
):
    sec = lax.axis_index("section")
    ten = lax.axis_index("tensor")
    blocks = a_ref.shape[1] // BLOCK
    steps = 2 * blocks
    cols = a_ref.shape[2]
    over_x = ten + 1 - 2 * (ten % 2)
    over_y = ten + 2 - 4 * (ten // 2)
    peers = (ten, over_x, over_y, 3 - ten)
    even = sec % 2 == 0
    top = sections - 2

    x_copies = [
        pltpu.make_async_copy(
            a_ref.at[0, pl.ds(k * BLOCK, BLOCK)], got.at[k, 0], x_sem.at[k]
        )
        for k in range(blocks)
    ]
    wq_copies, wkv_copies = [], []
    for r in range(4):
        part = pl.ds(pl.multiple_of(peers[r] * cols, cols), cols)
        wq_copies.append(
            pltpu.make_async_copy(
                wq_ref.at[0, part], weight.at[pl.ds(r * cols, cols), pl.ds(0, cols)], wq_sem.at[r]
            )
        )
        wkv_copies.append(
            pltpu.make_async_copy(wkv_ref.at[0, :, part], kv_raw.at[r], wkv_sem.at[r])
        )
    pool_copy = pltpu.make_async_copy(pool_ref, pool_rows.at[0], pool_sem)
    small_copies = [
        pltpu.make_async_copy(src, dst, small_sem.at[i])
        for i, (src, dst) in enumerate(
            ((gain_hbm, gain_ref), (seg_hbm, seg_ref), (ids_hbm, ids_ref), (len_hbm, len_ref))
        )
    ]
    for copy in small_copies:
        copy.start()

    barrier = pltpu.get_barrier_semaphore()
    for r in (1, 2, 3):
        pl.semaphore_signal(barrier, inc=1, device_id=(sec, peers[r]), device_id_type=MESH)

    def greet(condition, other):
        @pl.when(condition)
        def _():
            pl.semaphore_signal(barrier, inc=1, device_id=(other, ten), device_id_type=MESH)

    greet(sec > 0, sec - 1)
    greet(sec < sections - 1, sec + 1)
    greet(even & (sec > 1), sec - 2)
    greet(even & (sec < top), sec + 2)
    others = 3
    for condition in (sec > 0, sec < sections - 1, even & (sec > 1), even & (sec < top)):
        others = others + jnp.where(condition, 1, 0)
    pl.semaphore_wait(barrier, others)

    def remote(src, dst, send_sem, recv_sem, device):
        return pltpu.make_async_remote_copy(
            src_ref=src, dst_ref=dst, send_sem=send_sem, recv_sem=recv_sem,
            device_id=device, device_id_type=MESH,
        )

    def own_copy(src, b, way):
        return remote(
            src, got.at[b, 1 + way], own_send.at[b, way], own_recv.at[b, way],
            (sec, peers[1 + way]),
        )

    half = BLOCK // 2

    def forward_copy(b, way):
        rows = pl.ds(way * half, half)
        return remote(
            got.at[b, 1 + way, rows], got.at[b, 3, rows], fwd_send.at[b, way],
            fwd_recv.at[b, way], (sec, peers[2 - way]),
        )

    def hand_copy(k):
        return remote(
            result.at[k], got.at[blocks + k, 0], hand_send.at[k], hand_recv.at[k], (sec + 1, ten)
        )

    def sum_copy(k):
        return remote(below.at[k], above.at[k], sum_send.at[k], sum_recv.at[k], (sec - 2, ten))

    def gain_copy(r):
        return remote(
            gains.at[0], gains.at[r], gain_send.at[r - 1], gain_recv.at[r - 1], (sec, peers[r])
        )

    mate_copy = remote(pool_ref, pool_rows.at[1], mate_send, mate_recv, (sec - 1, ten))

    for k in range(2):
        for way in range(2):
            own_copy(a_ref.at[0, pl.ds(k * BLOCK, BLOCK)], k, way).start()
    for copy in wkv_copies + x_copies[:1] + wq_copies + x_copies[1:]:
        copy.start()

    @pl.when(even)
    def _():
        pool_copy.start()

    for copy in small_copies:
        copy.wait()
    gains[0] = jnp.broadcast_to(gain_ref[...], gains.shape[1:])
    for r in (1, 2, 3):
        gain_copy(r).start()

    @pl.when(sec % 2 == 1)
    def _():
        mate_copy.start()

    positions = lax.broadcasted_iota(jnp.int32, (1, blocks * BLOCK), 1)
    start = jnp.int32(0)
    slot = jnp.zeros_like(positions)
    source = jnp.zeros_like(positions)
    for j in range(slots):
        here = positions >= start
        slot = jnp.where(here, j, slot)
        source = jnp.where(here, ids_ref[j] * pool_ref.shape[1] - start + positions, source)
        start = start + len_ref[j]
    first_segments = seg_ref[pl.ds(sec, 1), :]
    prior_segments = seg_ref[pl.ds(jnp.maximum(sec - 1, 0), 1), :]
    second_segments = jnp.where(sec == 0, slot, prior_segments)
    for k in range(blocks):
        part = slice(k * BLOCK, (k + 1) * BLOCK)
        seg_rows[k] = first_segments[:, part]
        seg_rows[blocks + k] = second_segments[:, part]
        src_rows[k] = source[:, part] - sec * hosts_rows
    keys[...] = jnp.zeros_like(keys)
    values[...] = jnp.ones_like(values)

    def picked(k):
        index = lax.broadcasted_iota(jnp.int32, (2 * hosts_rows, BLOCK), 0)
        hit = (index == src_rows[k]).astype(jnp.float32).astype(jnp.bfloat16)
        rows = pool_rows[...].reshape(2 * hosts_rows, cols)
        return lax.dot_general(
            hit, rows, (((0,), (0,)), ((), ())), preferred_element_type=jnp.float32
        )

    def pass_down(k):
        sum_copy(k).wait_recv()
        below[k] = (picked(k) + above[k].astype(jnp.float32)).astype(jnp.bfloat16)
        sum_copy(k).start()

    middle = even & (sec > 0) & (sec < top)

    for r in range(4):
        wkv_copies[r].wait()
        weight[r * cols:(r + 1) * cols, cols:] = kv_raw[r].T

    late = jnp.minimum((top - sec) // 2, 2) - 1

    for copy in wq_copies:
        copy.wait()
    for r in (1, 2, 3):
        gain_copy(r).wait_recv()

    def forward(b):
        for way in range(2):
            own_copy(got.at[b, 0], b, way).wait_recv()
            forward_copy(b, way).start()

    def scaled(b, r):
        wide = got[b, r].astype(jnp.float32)
        gain_row = gains[r].astype(jnp.float32)[0:1]
        normed[:, r * cols:(r + 1) * cols] = (wide * gain_row).astype(jnp.bfloat16)
        return jnp.sum(wide * wide, axis=1, keepdims=True)

    def begin(b):
        @pl.when(b < blocks)
        def _():
            pltpu.make_async_copy(
                a_ref.at[0, pl.ds(0, BLOCK)], got.at[b, 0], x_sem.at[b]
            ).wait()

        squares[...] = scaled(b, 0) + scaled(b, 1) + scaled(b, 2)
        for low in range(0, cols + 2 * HEAD_DIM, 256):
            early[:, low:low + 256] = jnp.dot(
                normed[:, :3 * cols], weight[:3 * cols, low:low + 256],
                preferred_element_type=jnp.float32,
            )

    forward(0)
    for way in range(2):
        own_copy(a_ref.at[0, pl.ds(2 * BLOCK, BLOCK)], 2, way).start()
    begin(0)

    def step(b, carry):
        @pl.when(b + 1 < steps)
        def _():
            forward(b + 1)

        @pl.when(even & (b == 0))
        def _():
            pool_copy.wait()
            mate_copy.wait_recv()

            @pl.when(sec == top)
            def _():
                def send(k, carry):
                    below[k] = picked(k).astype(jnp.bfloat16)
                    sum_copy(k).start()
                    return carry

                lax.fori_loop(0, blocks, send, 0)

            @pl.when(middle)
            def _():
                pass_down(0)

        down = b - late

        @pl.when(middle & (b > 0) & (down >= 1) & (down < blocks))
        def _():
            pass_down(down)

        for way in range(2):
            forward_copy(b, way).wait_recv()
        diagonal = scaled(b, 3)
        scale = lax.rsqrt((squares[...] + diagonal) / D + norm_eps)

        def project(low):
            late_part = jnp.dot(
                normed[:, 3 * cols:], weight[3 * cols:, low:low + 256],
                preferred_element_type=jnp.float32,
            )
            return ((early[:, low:low + 256] + late_part) * scale).astype(jnp.bfloat16)

        keys[0:BLOCK] = keys[BLOCK:]
        values[0:BLOCK, :HEAD_DIM] = values[BLOCK:, :HEAD_DIM]
        keyval = project(cols)
        keys[BLOCK:] = keyval[:, :HEAD_DIM]
        values[BLOCK:, :HEAD_DIM] = keyval[:, HEAD_DIM:]
        for low in range(0, cols, 256):
            two = project(low)
            query[low // HEAD_DIM] = two[:, :HEAD_DIM]
            query[low // HEAD_DIM + 1] = two[:, HEAD_DIM:]

        seg_here = seg_rows[b]
        seg_before = jnp.where(b % blocks > 0, seg_rows[jnp.maximum(b - 1, 0)], -1)
        seg_down = jnp.broadcast_to(seg_here, (BLOCK, BLOCK)).T
        row = lax.broadcasted_iota(jnp.int32, (BLOCK, BLOCK), 0)
        col = lax.broadcasted_iota(jnp.int32, (BLOCK, BLOCK), 1)
        allowed = jnp.concatenate(
            [
                jnp.where(seg_down == seg_before, 1, 0),
                jnp.where((seg_down == seg_here) & (col <= row), 1, 0),
            ],
            axis=1,
        )
        allowed = (allowed > 0)[None]
        all_keys = keys[...]
        all_values = values[...]
        for low in range(0, cols // HEAD_DIM, AT_ONCE):
            scores = lax.dot_general(
                query[low:low + AT_ONCE].reshape(AT_ONCE * BLOCK, HEAD_DIM), all_keys,
                (((1,), (1,)), ((), ())), preferred_element_type=jnp.float32,
            ).reshape(AT_ONCE, BLOCK, 2 * BLOCK) * (HEAD_DIM ** (-0.5) * LOG2_E)
            scores = jnp.where(allowed, scores, masked_score)
            powers = jnp.exp2(scores - jnp.max(scores, axis=2, keepdims=True))
            summed = jnp.dot(
                powers.astype(jnp.bfloat16).reshape(AT_ONCE * BLOCK, 2 * BLOCK), all_values,
                preferred_element_type=jnp.float32,
            ).reshape(AT_ONCE, BLOCK, 2 * HEAD_DIM)
            context = summed[:, :, :HEAD_DIM] / summed[:, :, HEAD_DIM:]
            context = context.astype(jnp.bfloat16).astype(jnp.float32)
            for h in range(AT_ONCE):
                part = slice((low + h) * HEAD_DIM, (low + h + 1) * HEAD_DIM)
                result[b, :, part] = (
                    got[b, 0, :, part].astype(jnp.float32) + context[h]
                ).astype(jnp.bfloat16)

        rows = pl.ds(pl.multiple_of((b % blocks) * BLOCK, BLOCK), BLOCK)

        @pl.when(b < blocks)
        def _():
            @pl.when(sec < sections - 1)
            def _():
                hand_copy(b).start()

            pltpu.make_async_copy(result.at[b], out1_ref.at[0, rows], out_sem.at[b]).start()

        @pl.when(b >= blocks)
        def _():
            pltpu.make_async_copy(result.at[b], out2_ref.at[0, rows], out_sem.at[b]).start()

        ahead = b + 3

        @pl.when(ahead < blocks)
        def _():
            for way in range(2):
                own_copy(
                    a_ref.at[0, pl.ds(pl.multiple_of(ahead * BLOCK, BLOCK), BLOCK)], ahead, way
                ).start()

        @pl.when((ahead >= blocks) & (ahead < steps))
        def _():
            k = ahead - blocks

            @pl.when(sec > 0)
            def _():
                hand_copy(k).wait_recv()

            @pl.when(sec == 0)
            def _():
                sum_copy(k).wait_recv()
                got[ahead, 0] = (picked(k) + above[k].astype(jnp.float32)).astype(jnp.bfloat16)

            for way in range(2):
                own_copy(got.at[ahead, 0], ahead, way).start()

        @pl.when(b + 1 < steps)
        def _():
            begin(b + 1)

        return carry

    lax.fori_loop(0, steps, step, 0)

    def drain(b, carry):
        for way in range(2):
            own_copy(got.at[b, 0], b, way).wait_send()
            forward_copy(b, way).wait_send()
        pltpu.make_async_copy(result.at[b], out1_ref.at[0, pl.ds(0, BLOCK)], out_sem.at[b]).wait()

        @pl.when(b < blocks)
        def _():
            @pl.when(sec < sections - 1)
            def _():
                hand_copy(b).wait_send()

            @pl.when(even & (sec > 0))
            def _():
                sum_copy(b).wait_send()

        return carry

    lax.fori_loop(0, steps, drain, 0)
    for r in (1, 2, 3):
        gain_copy(r).wait_send()

    @pl.when(sec % 2 == 1)
    def _():
        mate_copy.wait_send()


def relay(sections, activations, gain, w_query, w_kv, segments, pool, row_ids, row_lengths):
    tokens, cols = activations.shape[1:]
    blocks = tokens // BLOCK
    steps = 2 * blocks
    hosts_rows = pool.shape[0] * pool.shape[1]
    dma = pltpu.SemaphoreType.DMA
    bf16 = jnp.bfloat16
    anywhere = pl.BlockSpec(memory_space=pl.ANY)
    hbm = pl.BlockSpec(memory_space=pltpu.HBM)
    return pl.pallas_call(
        functools.partial(relay_kernel, sections, hosts_rows, row_ids.shape[0]),
        out_shape=(
            jax.ShapeDtypeStruct(activations.shape, bf16),
            jax.ShapeDtypeStruct(activations.shape, bf16),
        ),
        in_specs=[hbm] * 8,
        out_specs=(anywhere, anywhere),
        scratch_shapes=[
            pltpu.VMEM(gain.shape, bf16),
            pltpu.VMEM(segments.shape, jnp.int32),
            pltpu.SMEM(row_ids.shape, jnp.int32),
            pltpu.SMEM(row_lengths.shape, jnp.int32),
            dma((4,)),
            pltpu.VMEM((steps, 4, BLOCK, cols), bf16),
            pltpu.VMEM((4 * cols, cols + 2 * HEAD_DIM), bf16),
            pltpu.VMEM((4, 2 * HEAD_DIM, cols), bf16),
            pltpu.VMEM((4, 16, cols), bf16),
            pltpu.VMEM((BLOCK, 4 * cols), bf16),
            pltpu.VMEM((BLOCK, cols + 2 * HEAD_DIM), jnp.float32),
            pltpu.VMEM((BLOCK, 1), jnp.float32),
            pltpu.VMEM((cols // HEAD_DIM, BLOCK, HEAD_DIM), bf16),
            pltpu.VMEM((2 * BLOCK, HEAD_DIM), bf16),
            pltpu.VMEM((2 * BLOCK, 2 * HEAD_DIM), bf16),
            pltpu.VMEM((steps, 1, BLOCK), jnp.int32),
            pltpu.VMEM((blocks, 1, BLOCK), jnp.int32),
            pltpu.VMEM((2, *pool.shape), bf16),
            pltpu.VMEM((blocks, BLOCK, cols), bf16),
            pltpu.VMEM((blocks, BLOCK, cols), bf16),
            pltpu.VMEM((steps, BLOCK, cols), bf16),
            dma((steps, 2)), dma((steps, 2)), dma((steps, 2)), dma((steps, 2)),
            dma((3,)), dma((3,)), dma((blocks,)), dma((blocks,)),
            dma((blocks,)), dma((4,)), dma((4,)), dma, dma, dma,
            dma((blocks,)), dma((blocks,)), dma((steps,)),
        ],
        compiler_params=pltpu.CompilerParams(
            collective_id=0, has_side_effects=True, vmem_limit_bytes=48 * 1024 * 1024
        ),
    )(
        *(
            pltpu.with_memory_space_constraint(argument, pltpu.HBM)
            for argument in (
                activations, gain, w_query, w_kv, segments, pool, row_ids, row_lengths
            )
        )
    )


def solution(mesh):
    square = (
        mesh.shape["tensor"] == KV_HEADS == 4
        and mesh.shape["section"] % 2 == 0
        and mesh.shape["section"] >= 4
    )
    body = functools.partial(relay, mesh.shape["section"]) if square else per_device
    return jax.shard_map(
        body,
        mesh=mesh,
        in_specs=(
            P("section", None, "tensor"),
            P("section", "tensor"),
            P("section", None, "tensor"),
            P("section", "tensor", None),
            P(),
            P("section", None, "tensor"),
            P(),
            P(),
        ),
        out_specs=(P("section", None, "tensor"), P("section", None, "tensor")),
        check_vma=False,
    )
```

```python
import functools

import jax
import jax.numpy as jnp
from jax import lax
from jax.experimental import pallas as pl
from jax.experimental.pallas import tpu as pltpu
from jax.sharding import PartitionSpec as P

D = 4096
HEADS = 32
KV_HEADS = 4
HEAD_DIM = 128


norm_eps = 1e-05
masked_score = -1e30


def partner_2(block, axis, distance):
    count = lax.axis_size(axis)
    route = []
    for low in range(count):
        high = low | 1 << distance
        if high != low and high < count:
            route += [(low, high), (high, low)]
    return lax.ppermute(block, axis, route)


def from_behind(block, axis, distance):
    devices = range(lax.axis_size(axis))
    route = [(i - distance, i) for i in devices if i - distance in devices]
    return lax.ppermute(block, axis, route)


def attend(inputs, gain_cols, query_weight, keyval_weight, seg_ids, tensor_index):
    row_count, col_count = inputs.shape
    wide_inputs = inputs.astype(jnp.float32)
    square_total = lax.psum(jnp.sum(wide_inputs * wide_inputs, axis=1), "tensor")
    row_scale = lax.rsqrt(square_total / D + norm_eps)
    normed = (wide_inputs * row_scale[:, None] * gain_cols.astype(jnp.float32)[None, :]).astype(
        jnp.bfloat16
    )
    part_cols = lax.all_gather(normed, "tensor", axis=1, tiled=True)
    query_part = jnp.dot(part_cols, query_weight, preferred_element_type=jnp.float32)
    keyval_part = lax.dot_general(
        keyval_weight, part_cols, (((1,), (1,)), ((), ())), preferred_element_type=jnp.float32
    )
    query = query_part.astype(jnp.bfloat16)
    keyval = keyval_part.astype(jnp.bfloat16)
    heads_here = query_weight.shape[1] // HEAD_DIM
    group_size = HEADS // KV_HEADS
    group_devices = group_size // heads_here
    head_block = keyval
    for bit_number in range(group_devices.bit_length() - 1):
        partner = partner_2(head_block, "tensor", bit_number)
        is_lower = tensor_index // (1 << bit_number) % 2 == 0
        head_block = jnp.where(
            is_lower,
            jnp.concatenate([head_block, partner], axis=0),
            jnp.concatenate([partner, head_block], axis=0),
        )
    keys_cols = head_block[:HEAD_DIM]
    values_cols = head_block[HEAD_DIM:]
    query_heads = query.reshape(row_count, heads_here, HEAD_DIM)
    scores = jnp.einsum(
        "rhd,ds->hrs", query_heads, keys_cols, preferred_element_type=jnp.float32
    ) * HEAD_DIM ** (-0.5)
    positions = jnp.arange(row_count, dtype=jnp.int32)
    allowed = (seg_ids[:, None] == seg_ids[None, :]) & (positions[None, :] <= positions[:, None])
    scores = jnp.where(allowed[None, :, :], scores, masked_score)
    weights = jax.nn.softmax(scores, axis=-1).astype(jnp.bfloat16)
    context = jnp.einsum("hrs,ds->rhd", weights, values_cols, preferred_element_type=jnp.float32)
    context = context.astype(jnp.bfloat16).reshape(row_count, col_count)
    return (wide_inputs + context.astype(jnp.float32)).astype(jnp.bfloat16)


def pick_rows(running, host_rows, source):
    flat_rows = host_rows.reshape(-1, host_rows.shape[2])
    inside = (source >= 0) & (source < flat_rows.shape[0])
    taken = jnp.take(flat_rows, jnp.clip(source, 0, flat_rows.shape[0] - 1), axis=0)
    return jnp.where(inside[:, None], taken, running)


def per_device(activations, gain, w_query, w_kv, segments, pool, row_ids, row_lengths):
    section_index = lax.axis_index("section")
    tensor_index = lax.axis_index("tensor")
    token_count = activations.shape[1]
    col_count = activations.shape[2]
    own_segments = lax.dynamic_index_in_dim(segments, section_index, 0, keepdims=False)
    after_first = attend(activations[0], gain[0], w_query[0], w_kv[0], own_segments, tensor_index)[
        None
    ]
    ends = jnp.cumsum(row_lengths)
    positions = jnp.arange(token_count, dtype=jnp.int32)
    slot = jnp.sum((positions[:, None] >= ends[None, :]).astype(jnp.int32), axis=1)
    slot_match = slot[:, None] == jnp.arange(row_ids.shape[0], dtype=jnp.int32)[None, :]
    slot_start = jnp.sum(jnp.where(slot_match, (ends - row_lengths)[None, :], 0), axis=1)
    slot_row = jnp.sum(jnp.where(slot_match, row_ids[None, :], 0), axis=1)
    source = slot_row * pool.shape[1] + positions - slot_start
    empty_rows = jnp.zeros((token_count, col_count), jnp.bfloat16)
    fresh = pick_rows(empty_rows, lax.all_gather(pool, "section", axis=0, tiled=True), source)
    handed = from_behind(after_first, "section", 1)
    second_inputs = jnp.where(section_index == 0, fresh[None], handed)
    prior_segments = lax.dynamic_index_in_dim(
        segments, jnp.maximum(section_index - 1, 0), 0, keepdims=False
    )
    second_segments = jnp.where(section_index == 0, slot, prior_segments)
    after_second = attend(
        second_inputs[0], gain[0], w_query[0], w_kv[0], second_segments, tensor_index
    )[None]
    return (after_first, after_second)


BLOCK = 128
AT_ONCE = 4
PIECES = 4
LOG2_E = 1.4426950408889634
MESH = pl.DeviceIdType.MESH


def relay_kernel(
    sections, hosts_rows, slots,
    a_ref, gain_hbm, wq_ref, wkv_ref, seg_hbm, pool_ref, ids_hbm, len_hbm,
    out1_ref, out2_ref,
    gain_ref, seg_ref, ids_ref, len_ref, small_sem, got, weight, kv_raw, gains, normed, early, squares, query, keys, values, seg_rows, src_rows,
    pool_rows, above, below, result,
    own_send, own_recv, fwd_send, fwd_recv, gain_send, gain_recv, hand_send, hand_recv,
    x_sem, wq_sem, wkv_sem, pool_sem, mate_send, mate_recv, sum_send, sum_recv, out_sem,
):
    sec = lax.axis_index("section")
    ten = lax.axis_index("tensor")
    blocks = a_ref.shape[1] // BLOCK
    steps = 2 * blocks
    cols = a_ref.shape[2]
    over_x = ten + 1 - 2 * (ten % 2)
    over_y = ten + 2 - 4 * (ten // 2)
    peers = (ten, over_x, over_y, 3 - ten)
    even = sec % 2 == 0
    top = sections - 2

    x_copies = [
        pltpu.make_async_copy(
            a_ref.at[0, pl.ds(k * BLOCK, BLOCK)], got.at[k, 0], x_sem.at[k]
        )
        for k in range(blocks)
    ]
    wq_copies, wkv_copies = [], []
    for r in range(4):
        part = pl.ds(pl.multiple_of(peers[r] * cols, cols), cols)
        wq_copies.append(
            pltpu.make_async_copy(
                wq_ref.at[0, part], weight.at[pl.ds(r * cols, cols), pl.ds(0, cols)], wq_sem.at[r]
            )
        )
        wkv_copies.append(
            pltpu.make_async_copy(wkv_ref.at[0, :, part], kv_raw.at[r], wkv_sem.at[r])
        )
    pool_copy = pltpu.make_async_copy(pool_ref, pool_rows.at[0], pool_sem)
    small_copies = [
        pltpu.make_async_copy(src, dst, small_sem.at[i])
        for i, (src, dst) in enumerate(
            ((gain_hbm, gain_ref), (seg_hbm, seg_ref), (ids_hbm, ids_ref), (len_hbm, len_ref))
        )
    ]
    for copy in small_copies:
        copy.start()

    barrier = pltpu.get_barrier_semaphore()
    for r in (1, 2, 3):
        pl.semaphore_signal(barrier, inc=1, device_id=(sec, peers[r]), device_id_type=MESH)

    def greet(condition, other):
        @pl.when(condition)
        def _():
            pl.semaphore_signal(barrier, inc=1, device_id=(other, ten), device_id_type=MESH)

    greet(sec > 0, sec - 1)
    greet(sec < sections - 1, sec + 1)
    greet(even & (sec > 1), sec - 2)
    greet(even & (sec < top), sec + 2)
    others = 3
    for condition in (sec > 0, sec < sections - 1, even & (sec > 1), even & (sec < top)):
        others = others + jnp.where(condition, 1, 0)
    pl.semaphore_wait(barrier, others)

    def remote(src, dst, send_sem, recv_sem, device):
        return pltpu.make_async_remote_copy(
            src_ref=src, dst_ref=dst, send_sem=send_sem, recv_sem=recv_sem,
            device_id=device, device_id_type=MESH,
        )

    def own_copy(src, b, way):
        return remote(
            src, got.at[b, 1 + way], own_send.at[b, way], own_recv.at[b, way],
            (sec, peers[1 + way]),
        )

    half = BLOCK // 2

    def forward_copy(b, way):
        rows = pl.ds(way * half, half)
        return remote(
            got.at[b, 1 + way, rows], got.at[b, 3, rows], fwd_send.at[b, way],
            fwd_recv.at[b, way], (sec, peers[2 - way]),
        )

    def hand_copy(k):
        return remote(
            result.at[k], got.at[blocks + k, 0], hand_send.at[k], hand_recv.at[k], (sec + 1, ten)
        )

    def sum_copy(k):
        return remote(below.at[k], above.at[k], sum_send.at[k], sum_recv.at[k], (sec - 2, ten))

    def gain_copy(r):
        return remote(
            gains.at[0], gains.at[r], gain_send.at[r - 1], gain_recv.at[r - 1], (sec, peers[r])
        )

    mate_copy = remote(pool_ref, pool_rows.at[1], mate_send, mate_recv, (sec - 1, ten))

    for k in range(2):
        for way in range(2):
            own_copy(a_ref.at[0, pl.ds(k * BLOCK, BLOCK)], k, way).start()
    for copy in wkv_copies + x_copies[:1] + wq_copies + x_copies[1:]:
        copy.start()

    @pl.when(even)
    def _():
        pool_copy.start()

    for copy in small_copies:
        copy.wait()
    gains[0] = jnp.broadcast_to(gain_ref[...], gains.shape[1:])
    for r in (1, 2, 3):
        gain_copy(r).start()

    @pl.when(sec % 2 == 1)
    def _():
        mate_copy.start()

    positions = lax.broadcasted_iota(jnp.int32, (1, blocks * BLOCK), 1)
    start = jnp.int32(0)
    slot = jnp.zeros_like(positions)
    source = jnp.zeros_like(positions)
    for j in range(slots):
        here = positions >= start
        slot = jnp.where(here, j, slot)
        source = jnp.where(here, ids_ref[j] * pool_ref.shape[1] - start + positions, source)
        start = start + len_ref[j]
    first_segments = seg_ref[pl.ds(sec, 1), :]
    prior_segments = seg_ref[pl.ds(jnp.maximum(sec - 1, 0), 1), :]
    second_segments = jnp.where(sec == 0, slot, prior_segments)
    for k in range(blocks):
        part = slice(k * BLOCK, (k + 1) * BLOCK)
        seg_rows[k] = first_segments[:, part]
        seg_rows[blocks + k] = second_segments[:, part]
        src_rows[k] = source[:, part] - sec * hosts_rows
    keys[...] = jnp.zeros_like(keys)
    values[...] = jnp.ones_like(values)

    def picked(k):
        index = lax.broadcasted_iota(jnp.int32, (2 * hosts_rows, BLOCK), 0)
        hit = (index == src_rows[k]).astype(jnp.float32).astype(jnp.bfloat16)
        rows = pool_rows[...].reshape(2 * hosts_rows, cols)
        return lax.dot_general(
            hit, rows, (((0,), (0,)), ((), ())), preferred_element_type=jnp.float32
        )

    def pass_down(k):
        sum_copy(k).wait_recv()
        below[k] = (picked(k) + above[k].astype(jnp.float32)).astype(jnp.bfloat16)
        sum_copy(k).start()

    middle = even & (sec > 0) & (sec < top)

    for r in range(4):
        wkv_copies[r].wait()
        weight[r * cols:(r + 1) * cols, cols:] = kv_raw[r].T

    late = jnp.minimum((top - sec) // 2, 2) - 1

    for copy in wq_copies:
        copy.wait()
    for r in (1, 2, 3):
        gain_copy(r).wait_recv()

    def forward(b):
        for way in range(2):
            own_copy(got.at[b, 0], b, way).wait_recv()
            forward_copy(b, way).start()

    def scaled(b, r):
        wide = got[b, r].astype(jnp.float32)
        gain_row = gains[r].astype(jnp.float32)[0:1]
        normed[:, r * cols:(r + 1) * cols] = (wide * gain_row).astype(jnp.bfloat16)
        return jnp.sum(wide * wide, axis=1, keepdims=True)

    def begin(b):
        @pl.when(b < blocks)
        def _():
            pltpu.make_async_copy(
                a_ref.at[0, pl.ds(0, BLOCK)], got.at[b, 0], x_sem.at[b]
            ).wait()

        squares[b % 2] = scaled(b, 0) + scaled(b, 1) + scaled(b, 2)
        for low in range(0, cols + 2 * HEAD_DIM, 256):
            early[b % 2, :, low:low + 256] = jnp.dot(
                normed[:, :3 * cols], weight[:3 * cols, low:low + 256],
                preferred_element_type=jnp.float32,
            )

    forward(0)
    for way in range(2):
        own_copy(a_ref.at[0, pl.ds(2 * BLOCK, BLOCK)], 2, way).start()
    begin(0)

    def step(b, carry):
        @pl.when(b + 1 < steps)
        def _():
            forward(b + 1)

        @pl.when(even & (b == 0))
        def _():
            pool_copy.wait()
            mate_copy.wait_recv()

            @pl.when(sec == top)
            def _():
                def send(k, carry):
                    below[k] = picked(k).astype(jnp.bfloat16)
                    sum_copy(k).start()
                    return carry

                lax.fori_loop(0, blocks, send, 0)

            @pl.when(middle)
            def _():
                pass_down(0)

        down = b - late

        @pl.when(middle & (b > 0) & (down >= 1) & (down < blocks))
        def _():
            pass_down(down)

        @pl.when(b + 1 < steps)
        def _():
            begin(b + 1)

        for way in range(2):
            forward_copy(b, way).wait_recv()
        diagonal = scaled(b, 3)
        scale = lax.rsqrt((squares[b % 2] + diagonal) / D + norm_eps)

        def project(low):
            late_part = jnp.dot(
                normed[:, 3 * cols:], weight[3 * cols:, low:low + 256],
                preferred_element_type=jnp.float32,
            )
            return ((early[b % 2, :, low:low + 256] + late_part) * scale).astype(jnp.bfloat16)

        keys[0:BLOCK] = keys[BLOCK:]
        values[0:BLOCK, :HEAD_DIM] = values[BLOCK:, :HEAD_DIM]
        keyval = project(cols)
        keys[BLOCK:] = keyval[:, :HEAD_DIM]
        values[BLOCK:, :HEAD_DIM] = keyval[:, HEAD_DIM:]
        for low in range(0, cols, 256):
            two = project(low)
            query[low // HEAD_DIM] = two[:, :HEAD_DIM]
            query[low // HEAD_DIM + 1] = two[:, HEAD_DIM:]

        seg_here = seg_rows[b]
        seg_before = jnp.where(b % blocks > 0, seg_rows[jnp.maximum(b - 1, 0)], -1)
        seg_down = jnp.broadcast_to(seg_here, (BLOCK, BLOCK)).T
        row = lax.broadcasted_iota(jnp.int32, (BLOCK, BLOCK), 0)
        col = lax.broadcasted_iota(jnp.int32, (BLOCK, BLOCK), 1)
        allowed = jnp.concatenate(
            [
                jnp.where(seg_down == seg_before, 1, 0),
                jnp.where((seg_down == seg_here) & (col <= row), 1, 0),
            ],
            axis=1,
        )
        allowed = (allowed > 0)[None]
        all_keys = keys[...]
        all_values = values[...]
        for low in range(0, cols // HEAD_DIM, AT_ONCE):
            scores = lax.dot_general(
                query[low:low + AT_ONCE].reshape(AT_ONCE * BLOCK, HEAD_DIM), all_keys,
                (((1,), (1,)), ((), ())), preferred_element_type=jnp.float32,
            ).reshape(AT_ONCE, BLOCK, 2 * BLOCK) * (HEAD_DIM ** (-0.5) * LOG2_E)
            scores = jnp.where(allowed, scores, masked_score)
            powers = jnp.exp2(scores - jnp.max(scores, axis=2, keepdims=True))
            summed = jnp.dot(
                powers.astype(jnp.bfloat16).reshape(AT_ONCE * BLOCK, 2 * BLOCK), all_values,
                preferred_element_type=jnp.float32,
            ).reshape(AT_ONCE, BLOCK, 2 * HEAD_DIM)
            context = summed[:, :, :HEAD_DIM] / summed[:, :, HEAD_DIM:]
            context = context.astype(jnp.bfloat16).astype(jnp.float32)
            for h in range(AT_ONCE):
                part = slice((low + h) * HEAD_DIM, (low + h + 1) * HEAD_DIM)
                result[b, :, part] = (
                    got[b, 0, :, part].astype(jnp.float32) + context[h]
                ).astype(jnp.bfloat16)

        rows = pl.ds(pl.multiple_of((b % blocks) * BLOCK, BLOCK), BLOCK)

        @pl.when(b < blocks)
        def _():
            @pl.when(sec < sections - 1)
            def _():
                hand_copy(b).start()

            pltpu.make_async_copy(result.at[b], out1_ref.at[0, rows], out_sem.at[b]).start()

        @pl.when(b >= blocks)
        def _():
            pltpu.make_async_copy(result.at[b], out2_ref.at[0, rows], out_sem.at[b]).start()

        ahead = b + 3

        @pl.when(ahead < blocks)
        def _():
            for way in range(2):
                own_copy(
                    a_ref.at[0, pl.ds(pl.multiple_of(ahead * BLOCK, BLOCK), BLOCK)], ahead, way
                ).start()

        @pl.when((ahead >= blocks) & (ahead < steps))
        def _():
            k = ahead - blocks

            @pl.when(sec > 0)
            def _():
                hand_copy(k).wait_recv()

            @pl.when(sec == 0)
            def _():
                sum_copy(k).wait_recv()
                got[ahead, 0] = (picked(k) + above[k].astype(jnp.float32)).astype(jnp.bfloat16)

            for way in range(2):
                own_copy(got.at[ahead, 0], ahead, way).start()

        return carry

    lax.fori_loop(0, steps, step, 0)

    def drain(b, carry):
        for way in range(2):
            own_copy(got.at[b, 0], b, way).wait_send()
            forward_copy(b, way).wait_send()
        pltpu.make_async_copy(result.at[b], out1_ref.at[0, pl.ds(0, BLOCK)], out_sem.at[b]).wait()

        @pl.when(b < blocks)
        def _():
            @pl.when(sec < sections - 1)
            def _():
                hand_copy(b).wait_send()

            @pl.when(even & (sec > 0))
            def _():
                sum_copy(b).wait_send()

        return carry

    lax.fori_loop(0, steps, drain, 0)
    for r in (1, 2, 3):
        gain_copy(r).wait_send()

    @pl.when(sec % 2 == 1)
    def _():
        mate_copy.wait_send()


def write_kernel(first_ref, second_ref, out1_ref, out2_ref, sems):
    copies = []
    for i, (src, dst) in enumerate(((first_ref, out1_ref), (second_ref, out2_ref))):
        rows = src.shape[1] // PIECES
        for j in range(PIECES):
            part = pl.ds(j * rows, rows)
            copies.append(
                pltpu.make_async_copy(src.at[0, part], dst.at[0, part], sems.at[i, j])
            )
    for copy in copies:
        copy.start()
    for copy in copies:
        copy.wait()


def write_out(first, second):
    hbm = pl.BlockSpec(memory_space=pltpu.HBM)
    anywhere = pl.BlockSpec(memory_space=pl.ANY)
    shape = jax.ShapeDtypeStruct(first.shape, first.dtype)
    return pl.pallas_call(
        write_kernel,
        out_shape=(shape, shape),
        in_specs=[anywhere, anywhere],
        out_specs=(hbm, hbm),
        scratch_shapes=[pltpu.SemaphoreType.DMA((2, PIECES))],
    )(first, second)


def relay(sections, activations, gain, w_query, w_kv, segments, pool, row_ids, row_lengths):
    tokens, cols = activations.shape[1:]
    blocks = tokens // BLOCK
    steps = 2 * blocks
    hosts_rows = pool.shape[0] * pool.shape[1]
    dma = pltpu.SemaphoreType.DMA
    bf16 = jnp.bfloat16
    anywhere = pl.BlockSpec(memory_space=pl.ANY)
    hbm = pl.BlockSpec(memory_space=pltpu.HBM)
    results = pl.pallas_call(
        functools.partial(relay_kernel, sections, hosts_rows, row_ids.shape[0]),
        out_shape=(
            jax.ShapeDtypeStruct(activations.shape, bf16),
            jax.ShapeDtypeStruct(activations.shape, bf16),
        ),
        in_specs=[hbm] * 8,
        out_specs=(anywhere, anywhere),
        scratch_shapes=[
            pltpu.VMEM(gain.shape, bf16),
            pltpu.VMEM(segments.shape, jnp.int32),
            pltpu.SMEM(row_ids.shape, jnp.int32),
            pltpu.SMEM(row_lengths.shape, jnp.int32),
            dma((4,)),
            pltpu.VMEM((steps, 4, BLOCK, cols), bf16),
            pltpu.VMEM((4 * cols, cols + 2 * HEAD_DIM), bf16),
            pltpu.VMEM((4, 2 * HEAD_DIM, cols), bf16),
            pltpu.VMEM((4, 16, cols), bf16),
            pltpu.VMEM((BLOCK, 4 * cols), bf16),
            pltpu.VMEM((2, BLOCK, cols + 2 * HEAD_DIM), jnp.float32),
            pltpu.VMEM((2, BLOCK, 1), jnp.float32),
            pltpu.VMEM((cols // HEAD_DIM, BLOCK, HEAD_DIM), bf16),
            pltpu.VMEM((2 * BLOCK, HEAD_DIM), bf16),
            pltpu.VMEM((2 * BLOCK, 2 * HEAD_DIM), bf16),
            pltpu.VMEM((steps, 1, BLOCK), jnp.int32),
            pltpu.VMEM((blocks, 1, BLOCK), jnp.int32),
            pltpu.VMEM((2, *pool.shape), bf16),
            pltpu.VMEM((blocks, BLOCK, cols), bf16),
            pltpu.VMEM((blocks, BLOCK, cols), bf16),
            pltpu.VMEM((steps, BLOCK, cols), bf16),
            dma((steps, 2)), dma((steps, 2)), dma((steps, 2)), dma((steps, 2)),
            dma((3,)), dma((3,)), dma((blocks,)), dma((blocks,)),
            dma((blocks,)), dma((4,)), dma((4,)), dma, dma, dma,
            dma((blocks,)), dma((blocks,)), dma((steps,)),
        ],
        compiler_params=pltpu.CompilerParams(
            collective_id=0, has_side_effects=True, vmem_limit_bytes=48 * 1024 * 1024
        ),
    )(
        *(
            pltpu.with_memory_space_constraint(argument, pltpu.HBM)
            for argument in (
                activations, gain, w_query, w_kv, segments, pool, row_ids, row_lengths
            )
        )
    )
    return write_out(*results)


def solution(mesh):
    square = (
        mesh.shape["tensor"] == KV_HEADS == 4
        and mesh.shape["section"] % 2 == 0
        and mesh.shape["section"] >= 4
    )
    body = functools.partial(relay, mesh.shape["section"]) if square else per_device
    return jax.shard_map(
        body,
        mesh=mesh,
        in_specs=(
            P("section", None, "tensor"),
            P("section", "tensor"),
            P("section", None, "tensor"),
            P("section", "tensor", None),
            P(),
            P("section", None, "tensor"),
            P(),
            P(),
        ),
        out_specs=(P("section", None, "tensor"), P("section", None, "tensor")),
        check_vma=False,
    )
```

```python
import functools

import jax
import jax.numpy as jnp
from jax import lax
from jax.experimental import pallas as pl
from jax.experimental.pallas import tpu as pltpu
from jax.sharding import PartitionSpec as P

D = 4096
HEADS = 32
KV_HEADS = 4
HEAD_DIM = 128


norm_eps = 1e-05
masked_score = -1e30


def partner_2(block, axis, distance):
    count = lax.axis_size(axis)
    route = []
    for low in range(count):
        high = low | 1 << distance
        if high != low and high < count:
            route += [(low, high), (high, low)]
    return lax.ppermute(block, axis, route)


def from_behind(block, axis, distance):
    devices = range(lax.axis_size(axis))
    route = [(i - distance, i) for i in devices if i - distance in devices]
    return lax.ppermute(block, axis, route)


def attend(inputs, gain_cols, query_weight, keyval_weight, seg_ids, tensor_index):
    row_count, col_count = inputs.shape
    wide_inputs = inputs.astype(jnp.float32)
    square_total = lax.psum(jnp.sum(wide_inputs * wide_inputs, axis=1), "tensor")
    row_scale = lax.rsqrt(square_total / D + norm_eps)
    normed = (wide_inputs * row_scale[:, None] * gain_cols.astype(jnp.float32)[None, :]).astype(
        jnp.bfloat16
    )
    part_cols = lax.all_gather(normed, "tensor", axis=1, tiled=True)
    query_part = jnp.dot(part_cols, query_weight, preferred_element_type=jnp.float32)
    keyval_part = lax.dot_general(
        keyval_weight, part_cols, (((1,), (1,)), ((), ())), preferred_element_type=jnp.float32
    )
    query = query_part.astype(jnp.bfloat16)
    keyval = keyval_part.astype(jnp.bfloat16)
    heads_here = query_weight.shape[1] // HEAD_DIM
    group_size = HEADS // KV_HEADS
    group_devices = group_size // heads_here
    head_block = keyval
    for bit_number in range(group_devices.bit_length() - 1):
        partner = partner_2(head_block, "tensor", bit_number)
        is_lower = tensor_index // (1 << bit_number) % 2 == 0
        head_block = jnp.where(
            is_lower,
            jnp.concatenate([head_block, partner], axis=0),
            jnp.concatenate([partner, head_block], axis=0),
        )
    keys_cols = head_block[:HEAD_DIM]
    values_cols = head_block[HEAD_DIM:]
    query_heads = query.reshape(row_count, heads_here, HEAD_DIM)
    scores = jnp.einsum(
        "rhd,ds->hrs", query_heads, keys_cols, preferred_element_type=jnp.float32
    ) * HEAD_DIM ** (-0.5)
    positions = jnp.arange(row_count, dtype=jnp.int32)
    allowed = (seg_ids[:, None] == seg_ids[None, :]) & (positions[None, :] <= positions[:, None])
    scores = jnp.where(allowed[None, :, :], scores, masked_score)
    weights = jax.nn.softmax(scores, axis=-1).astype(jnp.bfloat16)
    context = jnp.einsum("hrs,ds->rhd", weights, values_cols, preferred_element_type=jnp.float32)
    context = context.astype(jnp.bfloat16).reshape(row_count, col_count)
    return (wide_inputs + context.astype(jnp.float32)).astype(jnp.bfloat16)


def pick_rows(running, host_rows, source):
    flat_rows = host_rows.reshape(-1, host_rows.shape[2])
    inside = (source >= 0) & (source < flat_rows.shape[0])
    taken = jnp.take(flat_rows, jnp.clip(source, 0, flat_rows.shape[0] - 1), axis=0)
    return jnp.where(inside[:, None], taken, running)


def per_device(activations, gain, w_query, w_kv, segments, pool, row_ids, row_lengths):
    section_index = lax.axis_index("section")
    tensor_index = lax.axis_index("tensor")
    token_count = activations.shape[1]
    col_count = activations.shape[2]
    own_segments = lax.dynamic_index_in_dim(segments, section_index, 0, keepdims=False)
    after_first = attend(activations[0], gain[0], w_query[0], w_kv[0], own_segments, tensor_index)[
        None
    ]
    ends = jnp.cumsum(row_lengths)
    positions = jnp.arange(token_count, dtype=jnp.int32)
    slot = jnp.sum((positions[:, None] >= ends[None, :]).astype(jnp.int32), axis=1)
    slot_match = slot[:, None] == jnp.arange(row_ids.shape[0], dtype=jnp.int32)[None, :]
    slot_start = jnp.sum(jnp.where(slot_match, (ends - row_lengths)[None, :], 0), axis=1)
    slot_row = jnp.sum(jnp.where(slot_match, row_ids[None, :], 0), axis=1)
    source = slot_row * pool.shape[1] + positions - slot_start
    empty_rows = jnp.zeros((token_count, col_count), jnp.bfloat16)
    fresh = pick_rows(empty_rows, lax.all_gather(pool, "section", axis=0, tiled=True), source)
    handed = from_behind(after_first, "section", 1)
    second_inputs = jnp.where(section_index == 0, fresh[None], handed)
    prior_segments = lax.dynamic_index_in_dim(
        segments, jnp.maximum(section_index - 1, 0), 0, keepdims=False
    )
    second_segments = jnp.where(section_index == 0, slot, prior_segments)
    after_second = attend(
        second_inputs[0], gain[0], w_query[0], w_kv[0], second_segments, tensor_index
    )[None]
    return (after_first, after_second)


BLOCK = 128
AT_ONCE = 4
LOG2_E = 1.4426950408889634
MESH = pl.DeviceIdType.MESH


def relay_kernel(
    sections, hosts_rows, slots,
    a_ref, gain_hbm, wq_ref, wkv_ref, seg_hbm, pool_ref, ids_hbm, len_hbm,
    out1_ref, out2_ref,
    gain_ref, seg_ref, ids_ref, len_ref, small_sem, got, weight, kv_raw, gains, normed, early, squares, query, keys, values, seg_rows, src_rows,
    pool_rows, above, below, result,
    own_send, own_recv, fwd_send, fwd_recv, gain_send, gain_recv, hand_send, hand_recv,
    x_sem, wq_sem, wkv_sem, pool_sem, mate_send, mate_recv, sum_send, sum_recv, out_sem,
):
    sec = lax.axis_index("section")
    ten = lax.axis_index("tensor")
    blocks = a_ref.shape[1] // BLOCK
    steps = 2 * blocks
    cols = a_ref.shape[2]
    over_x = ten + 1 - 2 * (ten % 2)
    over_y = ten + 2 - 4 * (ten // 2)
    peers = (ten, over_x, over_y, 3 - ten)
    even = sec % 2 == 0
    top = sections - 2

    x_copies = [
        pltpu.make_async_copy(
            a_ref.at[0, pl.ds(k * BLOCK, BLOCK)], got.at[k, 0], x_sem.at[k]
        )
        for k in range(blocks)
    ]
    wq_copies, wkv_copies = [], []
    for r in range(4):
        part = pl.ds(pl.multiple_of(peers[r] * cols, cols), cols)
        wq_copies.append(
            pltpu.make_async_copy(
                wq_ref.at[0, part], weight.at[pl.ds(r * cols, cols), pl.ds(0, cols)], wq_sem.at[r]
            )
        )
        wkv_copies.append(
            pltpu.make_async_copy(wkv_ref.at[0, :, part], kv_raw.at[r], wkv_sem.at[r])
        )
    pool_copy = pltpu.make_async_copy(pool_ref, pool_rows.at[0], pool_sem)
    small_copies = [
        pltpu.make_async_copy(src, dst, small_sem.at[i])
        for i, (src, dst) in enumerate(
            ((gain_hbm, gain_ref), (seg_hbm, seg_ref), (ids_hbm, ids_ref), (len_hbm, len_ref))
        )
    ]
    for copy in small_copies:
        copy.start()

    barrier = pltpu.get_barrier_semaphore()
    for r in (1, 2, 3):
        pl.semaphore_signal(barrier, inc=1, device_id=(sec, peers[r]), device_id_type=MESH)

    def greet(condition, other):
        @pl.when(condition)
        def _():
            pl.semaphore_signal(barrier, inc=1, device_id=(other, ten), device_id_type=MESH)

    greet(sec > 0, sec - 1)
    greet(sec < sections - 1, sec + 1)
    greet(even & (sec > 1), sec - 2)
    greet(even & (sec < top), sec + 2)
    others = 3
    for condition in (sec > 0, sec < sections - 1, even & (sec > 1), even & (sec < top)):
        others = others + jnp.where(condition, 1, 0)
    pl.semaphore_wait(barrier, others)

    def remote(src, dst, send_sem, recv_sem, device):
        return pltpu.make_async_remote_copy(
            src_ref=src, dst_ref=dst, send_sem=send_sem, recv_sem=recv_sem,
            device_id=device, device_id_type=MESH,
        )

    def own_copy(src, b, way):
        return remote(
            src, got.at[b, 1 + way], own_send.at[b, way], own_recv.at[b, way],
            (sec, peers[1 + way]),
        )

    half = BLOCK // 2

    def forward_copy(b, way):
        rows = pl.ds(way * half, half)
        return remote(
            got.at[b, 1 + way, rows], got.at[b, 3, rows], fwd_send.at[b, way],
            fwd_recv.at[b, way], (sec, peers[2 - way]),
        )

    def hand_copy(k):
        return remote(
            result.at[k], got.at[blocks + k, 0], hand_send.at[k], hand_recv.at[k], (sec + 1, ten)
        )

    def sum_copy(k):
        return remote(below.at[k], above.at[k], sum_send.at[k], sum_recv.at[k], (sec - 2, ten))

    def gain_copy(r):
        return remote(
            gains.at[0], gains.at[r], gain_send.at[r - 1], gain_recv.at[r - 1], (sec, peers[r])
        )

    mate_copy = remote(pool_ref, pool_rows.at[1], mate_send, mate_recv, (sec - 1, ten))

    for k in range(2):
        for way in range(2):
            own_copy(a_ref.at[0, pl.ds(k * BLOCK, BLOCK)], k, way).start()
    for copy in wkv_copies + x_copies[:1] + wq_copies + x_copies[1:]:
        copy.start()

    @pl.when(even)
    def _():
        pool_copy.start()

    for copy in small_copies:
        copy.wait()
    gains[0] = jnp.broadcast_to(gain_ref[...], gains.shape[1:])
    for r in (1, 2, 3):
        gain_copy(r).start()

    @pl.when(sec % 2 == 1)
    def _():
        mate_copy.start()

    positions = lax.broadcasted_iota(jnp.int32, (1, blocks * BLOCK), 1)
    start = jnp.int32(0)
    slot = jnp.zeros_like(positions)
    source = jnp.zeros_like(positions)
    for j in range(slots):
        here = positions >= start
        slot = jnp.where(here, j, slot)
        source = jnp.where(here, ids_ref[j] * pool_ref.shape[1] - start + positions, source)
        start = start + len_ref[j]
    first_segments = seg_ref[pl.ds(sec, 1), :]
    prior_segments = seg_ref[pl.ds(jnp.maximum(sec - 1, 0), 1), :]
    second_segments = jnp.where(sec == 0, slot, prior_segments)
    for k in range(blocks):
        part = slice(k * BLOCK, (k + 1) * BLOCK)
        seg_rows[k] = first_segments[:, part]
        seg_rows[blocks + k] = second_segments[:, part]
        src_rows[k] = source[:, part] - sec * hosts_rows
    keys[...] = jnp.zeros_like(keys)
    values[...] = jnp.ones_like(values)

    def picked(k):
        index = lax.broadcasted_iota(jnp.int32, (2 * hosts_rows, BLOCK), 0)
        hit = (index == src_rows[k]).astype(jnp.float32).astype(jnp.bfloat16)
        rows = pool_rows[...].reshape(2 * hosts_rows, cols)
        return lax.dot_general(
            hit, rows, (((0,), (0,)), ((), ())), preferred_element_type=jnp.float32
        )

    def pass_down(k):
        sum_copy(k).wait_recv()
        below[k] = (picked(k) + above[k].astype(jnp.float32)).astype(jnp.bfloat16)
        sum_copy(k).start()

    middle = even & (sec > 0) & (sec < top)

    for r in range(4):
        wkv_copies[r].wait()
        weight[r * cols:(r + 1) * cols, cols:] = kv_raw[r].T

    late = jnp.minimum((top - sec) // 2, 2) - 1

    for copy in wq_copies:
        copy.wait()
    for r in (1, 2, 3):
        gain_copy(r).wait_recv()

    def forward(b):
        for way in range(2):
            own_copy(got.at[b, 0], b, way).wait_recv()
            forward_copy(b, way).start()

    def scaled(b, r):
        wide = got[b, r].astype(jnp.float32)
        gain_row = gains[r].astype(jnp.float32)[0:1]
        normed[:, r * cols:(r + 1) * cols] = (wide * gain_row).astype(jnp.bfloat16)
        return jnp.sum(wide * wide, axis=1, keepdims=True)

    def begin(b):
        @pl.when(b < blocks)
        def _():
            pltpu.make_async_copy(
                a_ref.at[0, pl.ds(0, BLOCK)], got.at[b, 0], x_sem.at[b]
            ).wait()

        squares[...] = scaled(b, 0) + scaled(b, 1) + scaled(b, 2)
        for low in range(0, cols + 2 * HEAD_DIM, 256):
            early[:, low:low + 256] = jnp.dot(
                normed[:, :3 * cols], weight[:3 * cols, low:low + 256],
                preferred_element_type=jnp.float32,
            )

    forward(0)

    @pl.when(even)
    def _():
        for way in range(2):
            own_copy(a_ref.at[0, pl.ds(2 * BLOCK, BLOCK)], 2, way).start()

    begin(0)

    def step(b, carry):
        @pl.when(b + 1 < steps)
        def _():
            forward(b + 1)

        @pl.when(even & (b == 0))
        def _():
            pool_copy.wait()
            mate_copy.wait_recv()

            @pl.when(sec == top)
            def _():
                def send(k, carry):
                    below[k] = picked(k).astype(jnp.bfloat16)
                    sum_copy(k).start()
                    return carry

                lax.fori_loop(0, blocks, send, 0)

            @pl.when(middle)
            def _():
                pass_down(0)

        down = b - late

        @pl.when(middle & (b > 0) & (down >= 1) & (down < blocks))
        def _():
            pass_down(down)

        for way in range(2):
            forward_copy(b, way).wait_recv()
        diagonal = scaled(b, 3)
        scale = lax.rsqrt((squares[...] + diagonal) / D + norm_eps)

        def project(low):
            late_part = jnp.dot(
                normed[:, 3 * cols:], weight[3 * cols:, low:low + 256],
                preferred_element_type=jnp.float32,
            )
            return ((early[:, low:low + 256] + late_part) * scale).astype(jnp.bfloat16)

        keys[0:BLOCK] = keys[BLOCK:]
        values[0:BLOCK, :HEAD_DIM] = values[BLOCK:, :HEAD_DIM]
        keyval = project(cols)
        keys[BLOCK:] = keyval[:, :HEAD_DIM]
        values[BLOCK:, :HEAD_DIM] = keyval[:, HEAD_DIM:]
        for low in range(0, cols, 256):
            two = project(low)
            query[low // HEAD_DIM] = two[:, :HEAD_DIM]
            query[low // HEAD_DIM + 1] = two[:, HEAD_DIM:]

        seg_here = seg_rows[b]
        seg_before = jnp.where(b % blocks > 0, seg_rows[jnp.maximum(b - 1, 0)], -1)
        seg_down = jnp.broadcast_to(seg_here, (BLOCK, BLOCK)).T
        row = lax.broadcasted_iota(jnp.int32, (BLOCK, BLOCK), 0)
        col = lax.broadcasted_iota(jnp.int32, (BLOCK, BLOCK), 1)
        allowed = jnp.concatenate(
            [
                jnp.where(seg_down == seg_before, 1, 0),
                jnp.where((seg_down == seg_here) & (col <= row), 1, 0),
            ],
            axis=1,
        )
        allowed = (allowed > 0)[None]
        all_keys = keys[...]
        all_values = values[...]
        for low in range(0, cols // HEAD_DIM, AT_ONCE):
            scores = lax.dot_general(
                query[low:low + AT_ONCE].reshape(AT_ONCE * BLOCK, HEAD_DIM), all_keys,
                (((1,), (1,)), ((), ())), preferred_element_type=jnp.float32,
            ).reshape(AT_ONCE, BLOCK, 2 * BLOCK) * (HEAD_DIM ** (-0.5) * LOG2_E)
            scores = jnp.where(allowed, scores, masked_score)
            powers = jnp.exp2(scores - jnp.max(scores, axis=2, keepdims=True))
            summed = jnp.dot(
                powers.astype(jnp.bfloat16).reshape(AT_ONCE * BLOCK, 2 * BLOCK), all_values,
                preferred_element_type=jnp.float32,
            ).reshape(AT_ONCE, BLOCK, 2 * HEAD_DIM)
            context = summed[:, :, :HEAD_DIM] / summed[:, :, HEAD_DIM:]
            context = context.astype(jnp.bfloat16).astype(jnp.float32)
            for h in range(AT_ONCE):
                part = slice((low + h) * HEAD_DIM, (low + h + 1) * HEAD_DIM)
                result[b, :, part] = (
                    got[b, 0, :, part].astype(jnp.float32) + context[h]
                ).astype(jnp.bfloat16)

        rows = pl.ds(pl.multiple_of((b % blocks) * BLOCK, BLOCK), BLOCK)

        @pl.when(b < blocks)
        def _():
            @pl.when(sec < sections - 1)
            def _():
                hand_copy(b).start()

            pltpu.make_async_copy(result.at[b], out1_ref.at[0, rows], out_sem.at[b]).start()

        @pl.when(b >= blocks)
        def _():
            pltpu.make_async_copy(result.at[b], out2_ref.at[0, rows], out_sem.at[b]).start()

        ahead = b + 3 - sec % 2

        @pl.when(ahead < blocks)
        def _():
            for way in range(2):
                own_copy(
                    a_ref.at[0, pl.ds(pl.multiple_of(ahead * BLOCK, BLOCK), BLOCK)], ahead, way
                ).start()

        @pl.when((ahead >= blocks) & (ahead < steps))
        def _():
            k = ahead - blocks

            @pl.when(sec > 0)
            def _():
                hand_copy(k).wait_recv()

            @pl.when(sec == 0)
            def _():
                sum_copy(k).wait_recv()
                got[ahead, 0] = (picked(k) + above[k].astype(jnp.float32)).astype(jnp.bfloat16)

            for way in range(2):
                own_copy(got.at[ahead, 0], ahead, way).start()

        @pl.when(b + 1 < steps)
        def _():
            begin(b + 1)

        return carry

    lax.fori_loop(0, steps, step, 0)

    def drain(b, carry):
        for way in range(2):
            own_copy(got.at[b, 0], b, way).wait_send()
            forward_copy(b, way).wait_send()
        pltpu.make_async_copy(result.at[b], out1_ref.at[0, pl.ds(0, BLOCK)], out_sem.at[b]).wait()

        @pl.when(b < blocks)
        def _():
            @pl.when(sec < sections - 1)
            def _():
                hand_copy(b).wait_send()

            @pl.when(even & (sec > 0))
            def _():
                sum_copy(b).wait_send()

        return carry

    lax.fori_loop(0, steps, drain, 0)
    for r in (1, 2, 3):
        gain_copy(r).wait_send()

    @pl.when(sec % 2 == 1)
    def _():
        mate_copy.wait_send()


def relay(sections, activations, gain, w_query, w_kv, segments, pool, row_ids, row_lengths):
    tokens, cols = activations.shape[1:]
    blocks = tokens // BLOCK
    steps = 2 * blocks
    hosts_rows = pool.shape[0] * pool.shape[1]
    dma = pltpu.SemaphoreType.DMA
    bf16 = jnp.bfloat16
    anywhere = pl.BlockSpec(memory_space=pl.ANY)
    hbm = pl.BlockSpec(memory_space=pltpu.HBM)
    return pl.pallas_call(
        functools.partial(relay_kernel, sections, hosts_rows, row_ids.shape[0]),
        out_shape=(
            jax.ShapeDtypeStruct(activations.shape, bf16),
            jax.ShapeDtypeStruct(activations.shape, bf16),
        ),
        in_specs=[hbm] * 8,
        out_specs=(anywhere, anywhere),
        scratch_shapes=[
            pltpu.VMEM(gain.shape, bf16),
            pltpu.VMEM(segments.shape, jnp.int32),
            pltpu.SMEM(row_ids.shape, jnp.int32),
            pltpu.SMEM(row_lengths.shape, jnp.int32),
            dma((4,)),
            pltpu.VMEM((steps, 4, BLOCK, cols), bf16),
            pltpu.VMEM((4 * cols, cols + 2 * HEAD_DIM), bf16),
            pltpu.VMEM((4, 2 * HEAD_DIM, cols), bf16),
            pltpu.VMEM((4, 16, cols), bf16),
            pltpu.VMEM((BLOCK, 4 * cols), bf16),
            pltpu.VMEM((BLOCK, cols + 2 * HEAD_DIM), jnp.float32),
            pltpu.VMEM((BLOCK, 1), jnp.float32),
            pltpu.VMEM((cols // HEAD_DIM, BLOCK, HEAD_DIM), bf16),
            pltpu.VMEM((2 * BLOCK, HEAD_DIM), bf16),
            pltpu.VMEM((2 * BLOCK, 2 * HEAD_DIM), bf16),
            pltpu.VMEM((steps, 1, BLOCK), jnp.int32),
            pltpu.VMEM((blocks, 1, BLOCK), jnp.int32),
            pltpu.VMEM((2, *pool.shape), bf16),
            pltpu.VMEM((blocks, BLOCK, cols), bf16),
            pltpu.VMEM((blocks, BLOCK, cols), bf16),
            pltpu.VMEM((steps, BLOCK, cols), bf16),
            dma((steps, 2)), dma((steps, 2)), dma((steps, 2)), dma((steps, 2)),
            dma((3,)), dma((3,)), dma((blocks,)), dma((blocks,)),
            dma((blocks,)), dma((4,)), dma((4,)), dma, dma, dma,
            dma((blocks,)), dma((blocks,)), dma((steps,)),
        ],
        compiler_params=pltpu.CompilerParams(
            collective_id=0, has_side_effects=True, vmem_limit_bytes=48 * 1024 * 1024
        ),
    )(
        *(
            pltpu.with_memory_space_constraint(argument, pltpu.HBM)
            for argument in (
                activations, gain, w_query, w_kv, segments, pool, row_ids, row_lengths
            )
        )
    )


def solution(mesh):
    square = (
        mesh.shape["tensor"] == KV_HEADS == 4
        and mesh.shape["section"] % 2 == 0
        and mesh.shape["section"] >= 4
    )
    body = functools.partial(relay, mesh.shape["section"]) if square else per_device
    return jax.shard_map(
        body,
        mesh=mesh,
        in_specs=(
            P("section", None, "tensor"),
            P("section", "tensor"),
            P("section", None, "tensor"),
            P("section", "tensor", None),
            P(),
            P("section", None, "tensor"),
            P(),
            P(),
        ),
        out_specs=(P("section", None, "tensor"), P("section", None, "tensor")),
        check_vma=False,
    )
```
